32 devices in a mesh: aux: 16 (over z, y, x), occ: 2 (over core).
Axes of the slice: x: 2, y: 2, z: 4, core: 2. Of those that a mesh axis runs over, the one named last changes fastest.
Arguments:
- three_index: bfloat16 [2, 64, 6, 128, 1024], P('occ', 'aux'), may hold values from -6 to 6
- fit_factor: bfloat16 [64, 128, 128], P('aux'), may hold values from -0.046875 to 0.046875
- slots: int32 [2, 64, 6], P('occ', 'aux'), may hold values from 0 to 15, all different within a row; in each aligned block of 4 rows (0 to 3, 4 to 7, ..., all dimensions but the last counted through in order) at most 2 rows name the same one
- owner: int32 [16], replicated, may hold values from 0 to 15, each once
Outputs:
- exchange_rows: float32 [16, 128, 2048], P('aux', None, 'occ')
The draws below stay inside these ranges and needn't reach their ends.
Inputs may be any that keep to these rules, and one draw needn't show every extreme that they name: `slots`: the 6 blocks of one row differ. In each aligned block of 4 rows (one device's auxiliary blocks for one occupied block) no basis block is listed more than 2 times, and some block exactly 2 times.
All inputs are finite; a program needn't handle non-finite values.
Results may differ from the reference program's by a relative error of at most 0.00054.
Values sent between devices are 32-bit elements; how exact they have to be, the bound alone decides.
No kernel may reach another device: no remote copies, remote signals or barrier semaphores. Data moves between devices by JAX's collectives and lax.ppermute only.
A program may use at most 128 MiB of HBM per device.

```python
import math
import jax
import jax.numpy as jnp
import numpy as np
from jax import lax

TILE = 128
OCC_DEV = 8
NAB_DEV = 4
SLOTS = 6
CAP = 2
NAUXB = 64
NBB = 16
N_OCC = 2


def steps_of(own_key, extent, pieces, smallest, high):
    level = 1.0
    for position, parts in pieces:
        draws = jax.random.uniform(jax.random.fold_in(jax.random.fold_in(own_key, 6), position), (parts,), jnp.float32, smallest / len(pieces), high / len(pieces))
        level = level * jnp.repeat(jnp.exp(draws), extent[position] // parts).reshape((-1,) + (1,) * (len(extent) - 1 - position))
    return level


def routed_block(own_key, own, number, rows, count, top, reach, skew):
    sequence = jax.random.permutation(own_key, count)
    heavy_load, ordinary = shares(count, rows * top, reach, skew, True), shares(count, rows * top, reach, skew, False)
    places = jnp.arange(count)

    def named(tallies, turn):
        used = int((tallies > 0).sum())
        fixed = max(1, used // 4)
        moved = fixed + (places - fixed + turn * (used - fixed)) % max(1, count - fixed)
        return jnp.zeros((count,), jnp.int32).at[sequence[jnp.where(places < fixed, places, moved)]].set(jnp.asarray(tallies, jnp.int32))

    tallies = jnp.where(number % 4 == 0, named(heavy_load, number // 4), named(ordinary, number - number // 4 - 1))
    mixed = jax.random.permutation(jax.random.fold_in(own, 3), count)
    donor, receiver = mixed[0:count // 2 * 2:2], mixed[1:count // 2 * 2:2]
    slack = jnp.minimum(tallies[donor] - 1, reach - tallies[receiver]) // 2
    slack = jnp.where((donor == sequence[0]) | (receiver == sequence[0]) | (tallies[receiver] == 0), 0, jnp.maximum(slack, 0))
    moved = jax.random.randint(jax.random.fold_in(own, 4), (count // 2,), 0, 1 << 20) % (slack + 1)
    tallies = tallies.at[donor].add(-moved).at[receiver].add(moved)
    labels = jnp.searchsorted(jnp.cumsum(tallies), jnp.arange(rows * top), side="right").astype(jnp.int32)
    listing = labels.reshape(top, rows).T
    listing = listing[jax.random.permutation(jax.random.fold_in(own, 1), rows)]
    turn = jax.random.randint(jax.random.fold_in(own, 2), (rows, 1), 0, top)
    return jnp.take_along_axis(listing, (jnp.arange(top)[None, :] + turn) % top, axis=1)


def shares(amount, total, limit, lean, full):
    portions = [(1 << 20) // math.isqrt(grade ** lean) + 1 for grade in range(1, amount + 1)]
    largest = limit if full else min(limit, max(-(-total // amount), total * portions[0] // sum(portions)))
    least = 1 if total - largest >= amount - 1 else 0
    given, rest = [largest] + [least] * (amount - 1), total - largest - least * (amount - 1)
    while rest > 0:
        candidates = [i for i in range(1, amount) if given[i] < largest] or [i for i in range(1, amount) if given[i] < limit]
        pool, budget = sum([portions[i] for i in candidates]), rest
        for i in candidates:
            addition = min(limit - given[i], max(1, budget * portions[i] // pool), rest)
            given[i] = given[i] + addition
            rest = rest - addition
    return np.array(given)


def noise(rng, shape, scale, bound, shards=(), kind=jnp.bfloat16):
    gain = steps_of(rng, shape, shards, -0.22, 0.18) if shards else 1.0
    values = jax.random.normal(rng, shape, jnp.float32) * scale * gain
    return jnp.minimum(jnp.maximum(values, -bound), bound).astype(kind)


def setup_inputs(seed: int = 0) -> dict:
    seeds = jax.random.split(jax.random.key(seed), 5)
    three_index = noise(seeds[0], (N_OCC, NAUXB, SLOTS, TILE, TILE * OCC_DEV), 1.0, 6.0, ((0, 2), (1, 16)))
    fit_factor = noise(seeds[1], (NAUXB, TILE, TILE), (TILE * TILE * OCC_DEV // 8) ** -0.5, 0.046875, ((0, 16),))
    slots_keys = jax.random.split(jax.random.fold_in(seeds[2], 1), N_OCC * NAUXB // NAB_DEV)
    slots_turns = jax.random.permutation(jax.random.fold_in(seeds[2], 3), N_OCC * NAUXB // NAB_DEV)
    slots = jax.vmap(lambda own, number: routed_block(jax.random.fold_in(seeds[2], 2), own, number, NAB_DEV, NBB, SLOTS, CAP, 2))(slots_keys, slots_turns).reshape((N_OCC, NAUXB, SLOTS))
    owner = jax.random.permutation(seeds[3], NBB).astype(jnp.int32)
    return {"three_index": three_index, "fit_factor": fit_factor, "slots": slots, "owner": owner}


def reference(three_index, fit_factor, slots, owner):
    n_occ, n_auxb, count_s, tile, width = three_index.shape
    orbitals = width // tile
    total_blocks = owner.shape[0]
    groups = n_auxb // NAB_DEV

    def step(total, index):
        occ_block = index // groups
        group = index % groups
        start = (group * NAB_DEV).astype(jnp.int32)
        zero = jnp.zeros((), jnp.int32)
        tiles = lax.dynamic_slice(three_index, (occ_block.astype(jnp.int32), start, zero, zero, zero), (1, NAB_DEV, count_s, tile, width))[0]
        factor = lax.dynamic_slice_in_dim(fit_factor, start, NAB_DEV, 0)
        blocks = lax.dynamic_slice(slots, (occ_block.astype(jnp.int32), start, zero), (1, NAB_DEV, count_s))[0]
        fitted = jnp.einsum("apq,asqf->aspf", factor.astype(jnp.float32), tiles.astype(jnp.float32)).astype(jnp.bfloat16)
        shaped = fitted.astype(jnp.float32).reshape(NAB_DEV, count_s, tile, tile, orbitals)
        contrib = jnp.einsum("aspni,atpmi->astnm", shaped, shaped)
        total = total.at[blocks[:, :, None], :, blocks[:, None, :], :].add(contrib)
        return total, None

    total = jnp.zeros((total_blocks, tile, total_blocks, tile), jnp.float32)
    total, unused = lax.scan(step, total, jnp.arange(n_occ * groups, dtype=jnp.int32))
    positions = jnp.zeros((total_blocks,), jnp.int32).at[owner].set(jnp.arange(total_blocks, dtype=jnp.int32))
    return total.reshape(total_blocks, tile, total_blocks * tile)[positions]
```

```python
import functools

import jax
import jax.numpy as jnp
from jax import lax
from jax.experimental import pallas as pl
from jax.experimental.pallas import tpu as pltpu
from jax.sharding import PartitionSpec as P

PLANE = 4


def pair_kernel(
    cfg, slots_ref, owner_ref, x_ref, fit_ref, send_s, send_k, keep_s, keep_k,
    xbuf, gbuf, fbuf, res, acc, ranked, insem, outsem,
):
    chips, cores, count_a, count_s, orbitals, rows, slices, sub, lines = cfg
    me = lax.axis_index("aux")
    core = lax.axis_index("occ")
    half = rows * cores
    for a in range(count_a):
        own = [owner_ref[slots_ref[a * count_s + s]] for s in range(count_s)]
        for s in range(count_s):
            rank = jnp.int32(0)
            for t in range(count_s):
                if t != s:
                    rank = rank + (own[t] < own[s]).astype(jnp.int32)
            place = a * count_s + rank
            ranked[place] = own[s]
            pltpu.make_async_copy(x_ref.at[a, s], xbuf.at[place], insem.at[place]).start()
    acc[...] = jnp.zeros_like(acc)

    def one(a, carry):
        base = a * count_s
        for p in range(count_s):
            pltpu.make_async_copy(x_ref.at[a, p], xbuf.at[base + p], insem.at[base + p]).wait()
            fitted = jnp.dot(fit_ref[a], xbuf[base + p], preferred_element_type=jnp.float32)
            gbuf[p] = fitted.T
            for i in range(orbitals):
                fbuf[p * 128:(p + 1) * 128, i * 128:(i + 1) * 128] = gbuf[
                    p, pl.ds(i, 128, stride=orbitals), :
                ].astype(jnp.bfloat16)
        for g in range(0, count_s, 2):
            res[g // 2, :, g * 128:] = lax.dot_general(
                fbuf[g * 128:(g + 2) * 128, :], fbuf[g * 128:, :],
                (((1,), (1,)), ((), ())), preferred_element_type=jnp.float32,
            )
        for p in range(count_s):
            for q in range(p, count_s):
                first, second = ranked[base + p], ranked[base + q]
                d = first ^ second
                unit = 1 + (d & (PLANE - 1)) * lines + (d >> 2)
                for h in range(2):
                    jr = (second if h else first) ^ me
                    u = 0 if (h and p == q) else unit
                    for o in range(cores):
                        for f in range(slices):
                            row = (p % 2) * 128 + h * half + (o ^ core) * rows + f * sub
                            tile = res[
                                p // 2, pl.ds(pl.multiple_of(row, sub), sub),
                                q * 128:(q + 1) * 128,
                            ]
                            bit = (jr >> f) & 1
                            rest = ((jr >> (f + 1)) << f) | (jr & ((1 << f) - 1))
                            acc[o, f, bit, rest, u] += tile
        return carry

    lax.fori_loop(0, count_a, one, 0)
    copies = []
    for o in range(cores):
        for f in range(slices):
            if o:
                copies.append((acc.at[o, f, 1], send_s.at[o - 1, f]))
                copies.append((acc.at[o, f, 0], send_k.at[o - 1, f]))
            else:
                copies.append((acc.at[o, f, 1], keep_s.at[f]))
                copies.append((acc.at[o, f, 0], keep_k.at[f]))
    copies = [pltpu.make_async_copy(a, b, outsem.at[i]) for i, (a, b) in enumerate(copies)]
    for c in copies:
        c.start()
    for c in copies:
        c.wait()


def place_kernel(cfg, owner_ref, *refs):
    chips, cores, rows, slices, sub, lines = cfg
    out, tiles = refs[-2], refs[-1]
    refs = refs[:-2]
    me = lax.axis_index("aux")
    core = lax.axis_index("occ")
    half = rows * cores
    per = len(refs) // cores
    for o in range(cores):
        line, own = refs[o * per], refs[o * per + 1]
        near, far = refs[o * per + 2], refs[o * per + 3]
        shift = (o ^ core) * rows
        for f in range(slices):
            for d in range(chips):
                dp, dz = d & (PLANE - 1), d >> 2
                if dp == 0:
                    mine = line[f, 1 + dz]
                    other = line[f, 0] if dz == 0 else line[f, lines + dz]
                else:
                    mine = own[f, dp - 1, dz]
                    other = near[dp - 1, f] if dz == 0 else far[dz - 1, dp - 1, f]
                top = (me >> (d.bit_length() - 1)) & 1 if d else 0
                at = shift + f * sub
                tiles[d, pl.ds(pl.multiple_of(top * half + at, sub), sub), :] = mine
                tiles[d, pl.ds(pl.multiple_of((1 - top) * half + at, sub), sub), :] = other
    blocks = chips // cores
    for i in range(blocks):
        k = owner_ref[core * blocks + i]
        d = k ^ me

        @pl.when(me <= k)
        def _():
            out[:, i * 128:(i + 1) * 128] = tiles[d]

        @pl.when(me > k)
        def _():
            out[:, i * 128:(i + 1) * 128] = tiles[d].T


def local(three_index, fit_factor, slots, owner):
    tiles = three_index[0]
    count_a, count_s, tile, width = tiles.shape
    orbitals = width // tile
    chips, cores = lax.axis_size("aux"), lax.axis_size("occ")
    lines = chips // PLANE
    rows = tile // 2 // cores
    slices = 2 if rows >= 16 else 1
    sub = rows // slices
    units = chips + 1
    inline = lines + 1
    f32 = jnp.float32

    def go(x, chip=0, core=0):
        if chip:
            return lax.ppermute(x, "aux", [(j, j ^ chip) for j in range(chips)])
        return lax.ppermute(x, "occ", [(j, j ^ core) for j in range(cores)])

    piece = (slices, chips // 2, units, sub, tile)
    any_spec = pl.BlockSpec(memory_space=pl.ANY)
    smem = pl.BlockSpec(memory_space=pltpu.SMEM)
    cfg = (chips, cores, count_a, count_s, orbitals, rows, slices, sub, lines)
    send_s, send_k, keep_s, keep_k = pl.pallas_call(
        functools.partial(pair_kernel, cfg),
        out_shape=[jax.ShapeDtypeStruct((cores - 1,) + piece, f32)] * 2
        + [jax.ShapeDtypeStruct(piece, f32)] * 2,
        in_specs=[smem, smem, any_spec, pl.BlockSpec(memory_space=pltpu.VMEM)],
        out_specs=[any_spec] * 4,
        scratch_shapes=[
            pltpu.VMEM((count_a * count_s, tile, width), jnp.bfloat16),
            pltpu.VMEM((count_s, width, tile), f32),
            pltpu.VMEM((count_s * tile, width), jnp.bfloat16),
            pltpu.VMEM((count_s // 2, 2 * tile, count_s * tile), f32),
            pltpu.VMEM((cores, slices, 2, chips // 2, units, sub, tile), f32),
            pltpu.SMEM((count_a * count_s,), jnp.int32),
            pltpu.SemaphoreType.DMA((count_a * count_s,)),
            pltpu.SemaphoreType.DMA((2 * cores * slices,)),
        ],
        compiler_params=pltpu.CompilerParams(vmem_limit_bytes=56 * 2**20),
        name="pairs",
    )(slots.reshape(-1), owner, tiles, fit_factor)

    got_s = [go(send_s[e - 1], core=e) for e in range(1, cores)]
    got_k = [go(send_k[e - 1], core=e) for e in range(1, cores)]

    def reduced(lo, hi):
        parts = []
        for f in range(slices):
            s = keep_s[f, :, lo:hi] + sum(g[f, :, lo:hi] for g in got_s)
            parts.append(go(s, chip=1 << f))
        nxt = []
        for f in range(slices):
            k = keep_k[f, :, lo:hi] + sum(g[f, :, lo:hi] for g in got_k)
            v = (k + parts[f]).reshape(lines, 2, hi - lo, sub, tile)
            nxt.append((v[:, 0], go(v[:, 1], chip=2 >> f)))
        return [a + b for a, b in nxt]

    pairs = jnp.stack(reduced(inline, units), axis=1)
    line = jnp.stack(reduced(0, inline), axis=1)

    got = [go(pairs[e], chip=e * PLANE) for e in range(1, lines)]
    own = pairs[0] + sum(got)
    own = own.reshape(slices, PLANE - 1, lines, sub, tile)

    def both(e):
        more = [line[e ^ dz, :, 1 + dz] for dz in range(1, lines)]
        return jnp.concatenate([line[e], jnp.stack(more, axis=1)], axis=1)

    got = [go(both(e), chip=e * PLANE) for e in range(1, lines)]
    line = both(0) + sum(got)

    near = [go(own[:, dp - 1], chip=dp) for dp in range(1, PLANE)]
    far = [
        go(jnp.stack([n[:, dz] for n in near]), chip=dz * PLANE) for dz in range(1, lines)
    ]
    near = jnp.stack([n[:, 0] for n in near])
    far = jnp.stack(far)
    mine = [line, own, near, far]
    every = list(mine)
    for e in range(1, cores):
        every += [go(m, core=e) for m in mine]

    vmem = pl.BlockSpec(memory_space=pltpu.VMEM)
    cfg = (chips, cores, rows, slices, sub, lines)
    result = pl.pallas_call(
        functools.partial(place_kernel, cfg),
        out_shape=jax.ShapeDtypeStruct((tile, chips // cores * tile), f32),
        in_specs=[smem] + [vmem] * len(every),
        out_specs=vmem,
        scratch_shapes=[pltpu.VMEM((chips, tile, tile), f32)],
        compiler_params=pltpu.CompilerParams(vmem_limit_bytes=24 * 2**20),
        name="place",
    )(owner, *every)
    return result[None]


def solution(mesh):
    placed = (P("occ", "aux", None, None, None), P("aux", None, None), P("occ", "aux", None), P())
    return jax.shard_map(
        local, mesh=mesh, in_specs=placed, out_specs=P("aux", None, "occ"), check_vma=False
    )
```

```python
import functools

import jax
import jax.numpy as jnp
import numpy as np
from jax import lax
from jax.experimental import pallas as pl
from jax.experimental.pallas import tpu as pltpu
from jax.sharding import PartitionSpec as P

PLANE = 4


class Sizes:
    def __init__(self, chips, cores, tile):
        self.chips, self.cores = chips, cores
        self.lines = chips // PLANE
        self.rows = tile // 2 // cores
        self.bits = chips.bit_length() - 1
        self.count = {
            "cross": (PLANE - 1) * (self.lines - 1), "plane": PLANE - 1, "line": self.lines + 1,
        }
        self.at, total = {}, 0
        for half in ("s", "k"):
            for name, n in self.count.items():
                size = chips // 2 * n * self.rows
                self.at[name, half] = (total, total + size)
                total += size
        self.sent, self.total = total // 2, total

    def order(self, name, core):
        low, high = [0, 1], list(range(2, self.bits))
        if core % 2:
            low, high = low[::-1], high[::-1]
        return high + low if name == "line" else low + high

    def table(self):
        out = np.zeros((self.chips, self.chips + 1, 2), np.int32)
        for j in range(self.chips):
            for unit in range(self.chips + 1):
                dz, dp = (unit // PLANE, unit % PLANE) if unit < self.chips else (-1, 0)
                if dp == 0:
                    name, i = "line", 1 + dz
                elif dz == 0:
                    name, i = "plane", dp - 1
                else:
                    name, i = "cross", (dp - 1) * (self.lines - 1) + dz - 1
                for parity in range(2):
                    place = 0
                    at = j ^ dp if name == "cross" else j
                    for bit in self.order(name, parity):
                        place = 2 * place + (at >> bit & 1)
                    half = self.chips // 2
                    base = self.at[name, "s" if place >= half else "k"][0]
                    place = (place % half) * self.count[name] + i
                    out[j, unit, parity] = base + place * self.rows
        return out.reshape(-1)


def pair_kernel(
    sz, slots_hbm, owner_hbm, table_hbm, x_ref, fit_hbm, keep, send,
    xbuf, both, gbuf, fbuf, res, fit_ref, slots_ref, owner_ref, table_ref, ranked, insem, smallsem,
):
    _, count_a, count_s, tile, width = x_ref.shape
    orbitals = width // tile
    me = lax.axis_index("aux")
    core = lax.axis_index("occ")
    half = tile // 2
    small = [
        pltpu.make_async_copy(a, b, smallsem.at[i]) for i, (a, b) in enumerate([
            (slots_hbm, slots_ref), (owner_hbm, owner_ref), (fit_hbm, fit_ref),
            (table_hbm, table_ref),
        ])
    ]
    for c in small:
        c.start()
    small[0].wait()
    small[1].wait()
    for a in range(count_a):
        own = [owner_ref[slots_ref[0, a, s]] for s in range(count_s)]
        for s in range(count_s):
            rank = jnp.int32(0)
            for t in range(count_s):
                if t != s:
                    rank = rank + (own[t] < own[s]).astype(jnp.int32)
            place = a * count_s + rank
            ranked[place] = own[s]
            pltpu.make_async_copy(
                x_ref.at[0, a, s], xbuf.at[pl.ds(pl.multiple_of(place * tile, tile), tile)],
                insem.at[place],
            ).start()
    keep[...] = jnp.zeros_like(keep)
    send[...] = jnp.zeros_like(send)
    both[...] = jnp.zeros_like(both)
    wide = 2 * tile
    span = wide // orbitals
    to = lax.broadcasted_iota(jnp.int32, (wide, wide), 0)
    of = lax.broadcasted_iota(jnp.int32, (wide, wide), 1)
    perm = (of == (to % span) * orbitals + to // span).astype(jnp.float32).astype(jnp.bfloat16)
    nt = (((1,), (1,)), ((), ()))
    small[2].wait()
    small[3].wait()

    def tiles_of(a):
        base = a * count_s
        slot = lax.rem(a, 2)
        both[:tile, :tile] = fit_ref[a]
        both[tile:, tile:] = fit_ref[a]
        for p in range(count_s):
            pltpu.make_async_copy(
                x_ref.at[0, a, p],
                xbuf.at[pl.ds(pl.multiple_of((base + p) * tile, tile), tile)],
                insem.at[base + p],
            ).wait()
        for g in range(0, count_s, 2):
            at = pl.multiple_of((base + g) * tile, tile)
            for b in range(width // wide):
                gbuf[g // 2, b * wide:(b + 1) * wide, :] = lax.dot_general(
                    perm, xbuf[pl.ds(at, wide), b * wide:(b + 1) * wide], nt,
                    preferred_element_type=jnp.float32,
                ).astype(jnp.bfloat16)
                yield
            for b in range(width // wide):
                fitted = lax.dot_general(
                    gbuf[g // 2, b * wide:(b + 1) * wide, :], both[...], nt,
                    preferred_element_type=jnp.float32,
                ).astype(jnp.bfloat16)
                for t in range(2):
                    top = (g + t) * tile + b * span
                    for i in range(orbitals):
                        fbuf[top:top + span, i * tile:(i + 1) * tile] = fitted[
                            i * span:(i + 1) * span, t * tile:(t + 1) * tile
                        ]
                yield
        for g in range(0, count_s, 2):
            res[slot, g // 2, :(g + 2) * tile, :] = lax.dot_general(
                fbuf[:(g + 2) * tile, :], fbuf[g * tile:(g + 2) * tile, :], nt,
                preferred_element_type=jnp.float32,
            )
            yield

    def add(a, p, q):
        base = a * count_s
        slot = lax.rem(a, 2)
        first, second = ranked[base + p], ranked[base + q]
        d = first ^ second
        todo = []
        for h in range(2):
            jr = (second if h else first) ^ me
            unit = sz.chips if (h and p == q) else d
            entry = (jr * (sz.chips + 1) + unit) * 2
            for o in range(sz.cores):
                of_core = o ^ core
                row = pl.multiple_of(table_ref[entry + (of_core & 1)], sz.rows)
                where = pl.ds(row, sz.rows)
                at = pl.multiple_of(p * tile + h * half + of_core * sz.rows, sz.rows)
                new = res[
                    slot, q // 2, pl.ds(at, sz.rows), (q % 2) * tile:(q % 2 + 1) * tile
                ]
                old = send[o - 1, where, :] if o else keep[where, :]
                todo.append((o, where, old + new))
        for o, where, value in todo:
            if o:
                send[o - 1, where, :] = value
            else:
                keep[where, :] = value

    pairs = [(p, q) for p in range(count_s) for q in range(p, count_s)]

    def both_of(a, carry):
        left = list(pairs)
        for _ in tiles_of(a):
            if left:
                add(a - 1, *left.pop())
        while left:
            add(a - 1, *left.pop())
        return carry

    for _ in tiles_of(jnp.int32(0)):
        pass
    lax.fori_loop(1, count_a, both_of, 0)
    for p, q in pairs:
        add(jnp.int32(count_a - 1), p, q)


def place_kernel(sz, owner_ref, *refs):
    out, tiles = refs[-2], refs[-1]
    refs = refs[:-2]
    me = lax.axis_index("aux")
    core = lax.axis_index("occ")
    tile = out.shape[0]
    half = tile // 2
    n_plane = sz.count["plane"]
    for o in range(sz.cores):
        own, far = refs[2 * o:2 * o + 2]
        shift = (o ^ core) * sz.rows
        for d in range(sz.chips):
            dp, dz = d % PLANE, d // PLANE
            if dp == 0:
                mine = own[n_plane + 1 + dz]
            elif dz == 0:
                mine = own[dp - 1]
            else:
                mine = far[(dp - 1) * sz.lines + dz]
            if d == 0:
                other = own[n_plane]
            elif dz == 0:
                other = far[(dp - 1) * sz.lines]
            else:
                other = far[n_plane * sz.lines + (dz - 1) * PLANE + dp]
            top = (me >> (d.bit_length() - 1)) & 1 if d else 0
            tiles[d, pl.ds(pl.multiple_of(top * half + shift, sz.rows), sz.rows), :] = mine
            tiles[d, pl.ds(pl.multiple_of((1 - top) * half + shift, sz.rows), sz.rows), :] = other
    blocks = sz.chips // sz.cores
    for i in range(blocks):
        k = owner_ref[core * blocks + i]
        d = k ^ me

        @pl.when(me <= k)
        def _():
            out[:, i * tile:(i + 1) * tile] = tiles[d]

        @pl.when(me > k)
        def _():
            out[:, i * tile:(i + 1) * tile] = tiles[d].T


def local(three_index, fit_factor, slots, owner):
    _, count_a, count_s, tile, width = three_index.shape
    chips, cores = lax.axis_size("aux"), lax.axis_size("occ")
    sz = Sizes(chips, cores, tile)
    lines, rows = sz.lines, sz.rows
    f32 = jnp.float32

    def go(x, chip=0, core=0):
        if chip:
            return lax.ppermute(x, "aux", [(j, j ^ chip) for j in range(chips)])
        return lax.ppermute(x, "occ", [(j, j ^ core) for j in range(cores)])

    vmem = pl.BlockSpec(memory_space=pltpu.VMEM)
    smem = pl.BlockSpec(memory_space=pltpu.SMEM)
    hbm = pl.BlockSpec(memory_space=pltpu.HBM)
    small = 4 * cores * sz.total * tile < 2**24
    space = pltpu.VMEM if small else jax.ShapeDtypeStruct
    keep, send = pl.pallas_call(
        functools.partial(pair_kernel, sz),
        out_shape=[
            space((sz.total, tile), f32), space((cores - 1, sz.total, tile), f32),
        ],
        in_specs=[hbm] * 5,
        out_specs=[vmem, vmem],
        scratch_shapes=[
            pltpu.VMEM((count_a * count_s * tile, width), jnp.bfloat16),
            pltpu.VMEM((2 * tile, 2 * tile), jnp.bfloat16),
            pltpu.VMEM((count_s // 2, width, 2 * tile), jnp.bfloat16),
            pltpu.VMEM((count_s * tile, width), jnp.bfloat16),
            pltpu.VMEM((2, count_s // 2, count_s * tile, 2 * tile), f32),
            pltpu.VMEM(fit_factor.shape, jnp.bfloat16),
            pltpu.SMEM(slots.shape, jnp.int32),
            pltpu.SMEM(owner.shape, jnp.int32),
            pltpu.SMEM((chips * (chips + 1) * 2,), jnp.int32),
            pltpu.SMEM((count_a * count_s,), jnp.int32),
            pltpu.SemaphoreType.DMA((count_a * count_s,)),
            pltpu.SemaphoreType.DMA((4,)),
        ],
        compiler_params=pltpu.CompilerParams(
            vmem_limit_bytes=40 * 2**20 if small else 58 * 2**20
        ),
        name="pairs",
    )(*[
        pltpu.with_memory_space_constraint(x, pltpu.HBM)
        for x in (slots, owner, jnp.asarray(sz.table()), three_index, fit_factor)
    ])

    first = sz.at["cross", "s"][1]
    cuts = [(0, first), (first, sz.sent), (sz.sent, sz.total)]
    got = [[go(send[e - 1, lo:hi], core=e) for e in range(1, cores)] for lo, hi in cuts]

    def step(x, name, k):
        pairs = []
        for j in range(chips):
            for c in range(cores):
                pairs.append((j * cores + c, (j ^ (1 << sz.order(name, c)[k])) * cores + c))
        return lax.ppermute(x, ("aux", "occ"), pairs)

    def total(terms):
        return functools.reduce(lambda a, b: a + b, terms)

    def terms(name, half):
        lo, hi = sz.at[name, half]
        shape = (chips // 2, sz.count[name], rows, tile)
        cut = 2 if half == "k" else int(name != "cross")
        off = cuts[cut][0]
        return [x.reshape(shape) for x in [keep[lo:hi]] + [g[lo - off:hi - off] for g in got[cut]]]

    parts, tail = {}, {}
    for k in range(sz.bits):
        for name in ("cross", "line", "plane"):
            if k:
                n = parts[name][0].shape[0] // 2
                sent, parts[name] = [x[n:] for x in parts[name]], [x[:n] for x in parts[name]]
            else:
                sent, parts[name] = terms(name, "s"), terms(name, "k")
            sent = total(sent)
            come = step(sent, name, k)
            tail[name, k] = come[-1:, -1:, -1:, -1:]
            parts[name].append(come)
    cross, line, plane = [total(parts[name])[0] for name in ("cross", "line", "plane")]
    cross = cross.reshape(PLANE - 1, lines - 1, rows, tile)
    near = [
        go(jnp.concatenate([plane[dp - 1:dp], cross[dp - 1]]), chip=dp) for dp in range(1, PLANE)
    ]
    far = [
        go(jnp.concatenate([line[1 + dz:2 + dz], cross[:, dz - 1]]), chip=dz * PLANE)
        for dz in range(1, lines)
    ]
    own = jnp.concatenate([plane, line])
    far = jnp.concatenate(near + far)
    every = [own, far]
    for e in range(1, cores):
        every += [go(own, core=e), go(far, core=e)]

    result = pl.pallas_call(
        functools.partial(place_kernel, sz),
        out_shape=jax.ShapeDtypeStruct((tile, chips // cores * tile), f32),
        in_specs=[smem] + [vmem] * len(every),
        out_specs=vmem,
        scratch_shapes=[pltpu.VMEM((chips, tile, tile), f32)],
        compiler_params=pltpu.CompilerParams(vmem_limit_bytes=24 * 2**20),
        name="place",
    )(owner, *every)
    return result[None]


def solution(mesh):
    placed = (P("occ", "aux", None, None, None), P("aux", None, None), P("occ", "aux", None), P())
    return jax.shard_map(
        local, mesh=mesh, in_specs=placed, out_specs=P("aux", None, "occ"), check_vma=False
    )
```

```python
import functools

import jax
import jax.numpy as jnp
import numpy as np
from jax import lax
from jax.experimental import pallas as pl
from jax.experimental.pallas import tpu as pltpu
from jax.sharding import PartitionSpec as P

PLANE = 4


class Sizes:
    def __init__(self, chips, cores, tile):
        self.chips, self.cores = chips, cores
        self.lines = chips // PLANE
        self.rows = tile // 2 // cores
        self.bits = chips.bit_length() - 1
        self.count = {
            "cross": (PLANE - 1) * (self.lines - 1), "plane": PLANE - 1, "line": self.lines + 1,
        }
        self.at, total = {}, 0
        for half in ("s", "k"):
            for name, n in self.count.items():
                size = chips // 2 * n * self.rows
                self.at[name, half] = (total, total + size)
                total += size
        self.sent, self.total = total // 2, total

    def order(self, name, core):
        low, high = [0, 1], list(range(2, self.bits))
        if core % 2:
            low, high = low[::-1], high[::-1]
        return high + low if name == "line" else low + high

    def table(self):
        out = np.zeros((self.chips, self.chips + 1, 2), np.int32)
        for j in range(self.chips):
            for unit in range(self.chips + 1):
                dz, dp = (unit // PLANE, unit % PLANE) if unit < self.chips else (-1, 0)
                for parity in range(2):
                    i = dp - 1 if dp == 3 else (dp - 1) ^ parity
                    if dp == 0:
                        name, i = "line", 1 + dz
                    elif dz == 0:
                        name = "plane"
                    else:
                        name, i = "cross", i * (self.lines - 1) + dz - 1
                    place = 0
                    at = j ^ dp if name == "cross" else j
                    for bit in self.order(name, parity):
                        place = 2 * place + (at >> bit & 1)
                    half = self.chips // 2
                    base = self.at[name, "s" if place >= half else "k"][0]
                    place = (place % half) * self.count[name] + i
                    out[j, unit, parity] = base + place * self.rows
        return out.reshape(-1)


def pair_kernel(
    sz, slots_hbm, owner_hbm, table_hbm, x_ref, fit_hbm, keep, send,
    xbuf, both, gbuf, fbuf, res, fit_ref, slots_ref, owner_ref, table_ref, ranked, insem, smallsem,
):
    _, count_a, count_s, tile, width = x_ref.shape
    orbitals = width // tile
    me = lax.axis_index("aux")
    core = lax.axis_index("occ")
    half = tile // 2
    small = [
        pltpu.make_async_copy(a, b, smallsem.at[i]) for i, (a, b) in enumerate([
            (slots_hbm, slots_ref), (owner_hbm, owner_ref), (fit_hbm, fit_ref),
            (table_hbm, table_ref),
        ])
    ]
    for c in small:
        c.start()
    small[0].wait()
    small[1].wait()
    for a in range(count_a):
        own = [owner_ref[slots_ref[0, a, s]] for s in range(count_s)]
        for s in range(count_s):
            rank = jnp.int32(0)
            for t in range(count_s):
                if t != s:
                    rank = rank + (own[t] < own[s]).astype(jnp.int32)
            place = a * count_s + rank
            ranked[place] = own[s]
            pltpu.make_async_copy(
                x_ref.at[0, a, s], xbuf.at[pl.ds(pl.multiple_of(place * tile, tile), tile)],
                insem.at[place],
            ).start()
    keep[...] = jnp.zeros_like(keep)
    send[...] = jnp.zeros_like(send)
    both[...] = jnp.zeros_like(both)
    wide = 2 * tile
    span = wide // orbitals
    to = lax.broadcasted_iota(jnp.int32, (wide, wide), 0)
    of = lax.broadcasted_iota(jnp.int32, (wide, wide), 1)
    perm = (of == (to % span) * orbitals + to // span).astype(jnp.float32).astype(jnp.bfloat16)
    nt = (((1,), (1,)), ((), ()))
    small[2].wait()
    small[3].wait()

    def tiles_of(a):
        base = a * count_s
        slot = lax.rem(a, 2)
        both[:tile, :tile] = fit_ref[a]
        both[tile:, tile:] = fit_ref[a]
        for p in range(count_s):
            pltpu.make_async_copy(
                x_ref.at[0, a, p],
                xbuf.at[pl.ds(pl.multiple_of((base + p) * tile, tile), tile)],
                insem.at[base + p],
            ).wait()
        for g in range(0, count_s, 2):
            at = pl.multiple_of((base + g) * tile, tile)
            for b in range(width // wide):
                gbuf[g // 2, b * wide:(b + 1) * wide, :] = lax.dot_general(
                    perm, xbuf[pl.ds(at, wide), b * wide:(b + 1) * wide], nt,
                    preferred_element_type=jnp.float32,
                ).astype(jnp.bfloat16)
                yield
            for b in range(width // wide):
                fitted = lax.dot_general(
                    gbuf[g // 2, b * wide:(b + 1) * wide, :], both[...], nt,
                    preferred_element_type=jnp.float32,
                ).astype(jnp.bfloat16)
                for t in range(2):
                    top = (g + t) * tile + b * span
                    for i in range(orbitals):
                        fbuf[top:top + span, i * tile:(i + 1) * tile] = fitted[
                            i * span:(i + 1) * span, t * tile:(t + 1) * tile
                        ]
                yield
        for g in range(0, count_s, 2):
            res[slot, g // 2, :(g + 2) * tile, :] = lax.dot_general(
                fbuf[:(g + 2) * tile, :], fbuf[g * tile:(g + 2) * tile, :], nt,
                preferred_element_type=jnp.float32,
            )
            yield

    def add(a, p, q):
        base = a * count_s
        slot = lax.rem(a, 2)
        first, second = ranked[base + p], ranked[base + q]
        d = first ^ second
        todo = []
        for h in range(2):
            jr = (second if h else first) ^ me
            unit = sz.chips if (h and p == q) else d
            entry = (jr * (sz.chips + 1) + unit) * 2
            for o in range(sz.cores):
                of_core = o ^ core
                row = pl.multiple_of(table_ref[entry + (of_core & 1)], sz.rows)
                where = pl.ds(row, sz.rows)
                at = pl.multiple_of(p * tile + h * half + of_core * sz.rows, sz.rows)
                new = res[
                    slot, q // 2, pl.ds(at, sz.rows), (q % 2) * tile:(q % 2 + 1) * tile
                ]
                old = send[o - 1, where, :] if o else keep[where, :]
                todo.append((o, where, old + new))
        for o, where, value in todo:
            if o:
                send[o - 1, where, :] = value
            else:
                keep[where, :] = value

    pairs = [(p, q) for p in range(count_s) for q in range(p, count_s)]

    def both_of(a, carry):
        left = list(pairs)
        for _ in tiles_of(a):
            if left:
                add(a - 1, *left.pop())
        while left:
            add(a - 1, *left.pop())
        return carry

    for _ in tiles_of(jnp.int32(0)):
        pass
    lax.fori_loop(1, count_a, both_of, 0)
    for p, q in pairs:
        add(jnp.int32(count_a - 1), p, q)


def place_kernel(sz, owner_ref, *refs):
    out, tiles = refs[-2], refs[-1]
    refs = refs[:-2]
    me = lax.axis_index("aux")
    core = lax.axis_index("occ")
    tile = out.shape[0]
    half = tile // 2
    n_plane = sz.count["plane"]
    for o in range(sz.cores):
        own, far = refs[2 * o:2 * o + 2]
        shift = (o ^ core) * sz.rows
        parity = (o ^ core) & 1
        for d in range(sz.chips):
            dp, dz = d % PLANE, d // PLANE
            i = dp - 1 if dp == 3 else (dp - 1) ^ parity
            if dp == 0:
                mine = own[n_plane + 1 + dz]
            elif dz == 0:
                mine = own[i]
            else:
                mine = far[i * sz.lines + dz]
            if d == 0:
                other = own[n_plane]
            elif dz == 0:
                other = far[i * sz.lines]
            else:
                other = far[n_plane * sz.lines + (dz - 1) * PLANE + (1 + i if dp else 0)]
            top = (me >> (d.bit_length() - 1)) & 1 if d else 0
            tiles[d, pl.ds(pl.multiple_of(top * half + shift, sz.rows), sz.rows), :] = mine
            tiles[d, pl.ds(pl.multiple_of((1 - top) * half + shift, sz.rows), sz.rows), :] = other
    blocks = sz.chips // sz.cores
    for i in range(blocks):
        k = owner_ref[core * blocks + i]
        d = k ^ me

        @pl.when(me <= k)
        def _():
            out[:, i * tile:(i + 1) * tile] = tiles[d]

        @pl.when(me > k)
        def _():
            out[:, i * tile:(i + 1) * tile] = tiles[d].T


def local(three_index, fit_factor, slots, owner):
    _, count_a, count_s, tile, width = three_index.shape
    chips, cores = lax.axis_size("aux"), lax.axis_size("occ")
    sz = Sizes(chips, cores, tile)
    lines, rows = sz.lines, sz.rows
    f32 = jnp.float32

    def go(x, chip=0, core=0):
        if chip:
            return lax.ppermute(x, "aux", [(j, j ^ chip) for j in range(chips)])
        return lax.ppermute(x, "occ", [(j, j ^ core) for j in range(cores)])

    vmem = pl.BlockSpec(memory_space=pltpu.VMEM)
    smem = pl.BlockSpec(memory_space=pltpu.SMEM)
    hbm = pl.BlockSpec(memory_space=pltpu.HBM)
    small = 4 * cores * sz.total * tile < 2**24
    space = pltpu.VMEM if small else jax.ShapeDtypeStruct
    keep, send = pl.pallas_call(
        functools.partial(pair_kernel, sz),
        out_shape=[
            space((sz.total, tile), f32), space((cores - 1, sz.total, tile), f32),
        ],
        in_specs=[hbm] * 5,
        out_specs=[vmem, vmem],
        scratch_shapes=[
            pltpu.VMEM((count_a * count_s * tile, width), jnp.bfloat16),
            pltpu.VMEM((2 * tile, 2 * tile), jnp.bfloat16),
            pltpu.VMEM((count_s // 2, width, 2 * tile), jnp.bfloat16),
            pltpu.VMEM((count_s * tile, width), jnp.bfloat16),
            pltpu.VMEM((2, count_s // 2, count_s * tile, 2 * tile), f32),
            pltpu.VMEM(fit_factor.shape, jnp.bfloat16),
            pltpu.SMEM(slots.shape, jnp.int32),
            pltpu.SMEM(owner.shape, jnp.int32),
            pltpu.SMEM((chips * (chips + 1) * 2,), jnp.int32),
            pltpu.SMEM((count_a * count_s,), jnp.int32),
            pltpu.SemaphoreType.DMA((count_a * count_s,)),
            pltpu.SemaphoreType.DMA((4,)),
        ],
        compiler_params=pltpu.CompilerParams(
            vmem_limit_bytes=40 * 2**20 if small else 58 * 2**20
        ),
        name="pairs",
    )(*[
        pltpu.with_memory_space_constraint(x, pltpu.HBM)
        for x in (slots, owner, jnp.asarray(sz.table()), three_index, fit_factor)
    ])

    first = sz.at["cross", "s"][1]
    cuts = [(0, first), (first, sz.sent), (sz.sent, sz.total)]
    got = []
    for lo, hi in cuts:
        moved = []
        for e in range(1, cores):
            x = send[e - 1, lo:hi]
            if got:
                x = x + 0 * got[0][e - 1][:1]
            moved.append(go(x, core=e))
        got.append(moved)

    def step(x, name, k):
        pairs = []
        for j in range(chips):
            for c in range(cores):
                pairs.append((j * cores + c, (j ^ (1 << sz.order(name, c)[k])) * cores + c))
        return lax.ppermute(x, ("aux", "occ"), pairs)

    def total(terms):
        return functools.reduce(lambda a, b: a + b, terms)

    def terms(name, half):
        lo, hi = sz.at[name, half]
        shape = (chips // 2, sz.count[name], rows, tile)
        cut = 2 if half == "k" else int(name != "cross")
        off = cuts[cut][0]
        return [x.reshape(shape) for x in [keep[lo:hi]] + [g[lo - off:hi - off] for g in got[cut]]]

    parts, before = {}, None
    for k in range(sz.bits):
        for name in ("cross", "line", "plane"):
            if k:
                n = parts[name][0].shape[0] // 2
                sent, parts[name] = [x[n:] for x in parts[name]], [x[:n] for x in parts[name]]
            else:
                sent, parts[name] = terms(name, "s"), terms(name, "k")
            sent = total(sent)
            if before is not None:
                sent = sent + 0 * before[:sent.shape[0], :1]
            before = sent
            come = step(sent, name, k)
            parts[name].append(come)
    cross = total(parts["cross"])[0]
    line = total(parts["line"])[0] + 0 * cross[:1]
    plane = total(parts["plane"])[0] + 0 * line[:1]
    cross = cross.reshape(PLANE - 1, lines - 1, rows, tile)
    near = [jnp.concatenate([plane[i:i + 1], cross[i]]) for i in range(PLANE - 1)]
    far = [
        jnp.concatenate([line[1 + dz:2 + dz], cross[:, dz - 1]]) for dz in range(1, lines)
    ]
    sent = jnp.stack([near[0], near[2]])
    far = [go(x, chip=dz * PLANE) for dz, x in enumerate(far, 1)]
    come = step(sent, "plane", 0)
    last = step(jnp.stack([near[1], come[1]]), "plane", 1)
    near = [come[0], last[0], last[1]]
    own = jnp.concatenate([plane, line])
    far = jnp.concatenate(near + far)
    every = [own, far]
    for e in range(1, cores):
        every += [go(own, core=e), go(far, core=e)]

    result = pl.pallas_call(
        functools.partial(place_kernel, sz),
        out_shape=jax.ShapeDtypeStruct((tile, chips // cores * tile), f32),
        in_specs=[smem] + [vmem] * len(every),
        out_specs=vmem,
        scratch_shapes=[pltpu.VMEM((chips, tile, tile), f32)],
        compiler_params=pltpu.CompilerParams(vmem_limit_bytes=24 * 2**20),
        name="place",
    )(owner, *every)
    return result[None]


def solution(mesh):
    placed = (P("occ", "aux", None, None, None), P("aux", None, None), P("occ", "aux", None), P())
    return jax.shard_map(
        local, mesh=mesh, in_specs=placed, out_specs=P("aux", None, "occ"), check_vma=False
    )
```

```python
import functools

import jax
import jax.numpy as jnp
import numpy as np
from jax import lax
from jax.experimental import pallas as pl
from jax.experimental.pallas import tpu as pltpu
from jax.sharding import PartitionSpec as P

PLANE = 4


class Sizes:
    def __init__(self, chips, cores, tile):
        self.chips, self.cores = chips, cores
        self.lines = chips // PLANE
        self.rows = tile // 2 // cores
        self.bits = chips.bit_length() - 1
        self.count = {
            "cross": (PLANE - 1) * (self.lines - 1), "plane": PLANE - 1, "line": self.lines + 1,
        }
        self.at, total = {}, 0
        for half in ("s", "k"):
            for name, n in self.count.items():
                size = chips // 2 * n * self.rows
                self.at[name, half] = (total, total + size)
                total += size
        self.sent, self.total = total // 2, total

    def order(self, name, core):
        low, high = [0, 1], list(range(2, self.bits))
        if core % 2:
            low, high = low[::-1], high[::-1]
        return high + low if name == "line" else low + high

    def place(self, d, bits, parity):
        if parity and d >= 0:
            return sum((d >> b & 1) << (bits - 1 - b) for b in range(bits))
        return d

    def table(self):
        out = np.zeros((self.chips, self.chips + 1, 2), np.int32)
        for j in range(self.chips):
            for unit in range(self.chips + 1):
                dz, dp = (unit // PLANE, unit % PLANE) if unit < self.chips else (-1, 0)
                for parity in range(2):
                    p, q = self.place(dp, 2, parity), self.place(dz, self.bits - 2, parity)
                    if dp == 0:
                        name, i = "line", 1 + q
                    elif dz == 0:
                        name, i = "plane", p - 1
                    else:
                        name, i = "cross", (p - 1) * (self.lines - 1) + q - 1
                    row = 0
                    at = j ^ dp if name == "cross" else j
                    for bit in self.order(name, parity):
                        row = 2 * row + (at >> bit & 1)
                    half = self.chips // 2
                    base = self.at[name, "s" if row >= half else "k"][0]
                    row = (row % half) * self.count[name] + i
                    out[j, unit, parity] = base + row * self.rows
        return out.reshape(-1)


def pair_kernel(
    sz, slots_hbm, owner_hbm, table_hbm, x_ref, fit_hbm, keep, send,
    xbuf, both, gbuf, fbuf, res, fit_ref, slots_ref, owner_ref, table_ref, ranked, insem, smallsem,
):
    _, count_a, count_s, tile, width = x_ref.shape
    orbitals = width // tile
    me = lax.axis_index("aux")
    core = lax.axis_index("occ")
    half = tile // 2
    small = [
        pltpu.make_async_copy(a, b, smallsem.at[i]) for i, (a, b) in enumerate([
            (slots_hbm, slots_ref), (owner_hbm, owner_ref), (fit_hbm, fit_ref),
            (table_hbm, table_ref),
        ])
    ]
    for c in small:
        c.start()
    small[0].wait()
    small[1].wait()
    for a in range(count_a):
        own = [owner_ref[slots_ref[0, a, s]] for s in range(count_s)]
        for s in range(count_s):
            rank = jnp.int32(0)
            for t in range(count_s):
                if t != s:
                    rank = rank + (own[t] < own[s]).astype(jnp.int32)
            place = a * count_s + rank
            ranked[place] = own[s]
            pltpu.make_async_copy(
                x_ref.at[0, a, s], xbuf.at[pl.ds(pl.multiple_of(place * tile, tile), tile)],
                insem.at[place],
            ).start()
    keep[...] = jnp.zeros_like(keep)
    send[...] = jnp.zeros_like(send)
    both[...] = jnp.zeros_like(both)
    wide = 2 * tile
    span = wide // orbitals
    to = lax.broadcasted_iota(jnp.int32, (wide, wide), 0)
    of = lax.broadcasted_iota(jnp.int32, (wide, wide), 1)
    perm = (of == (to % span) * orbitals + to // span).astype(jnp.float32).astype(jnp.bfloat16)
    nt = (((1,), (1,)), ((), ()))
    small[2].wait()
    small[3].wait()

    def tiles_of(a):
        base = a * count_s
        slot = lax.rem(a, 2)
        both[:tile, :tile] = fit_ref[a]
        both[tile:, tile:] = fit_ref[a]
        for p in range(count_s):
            pltpu.make_async_copy(
                x_ref.at[0, a, p],
                xbuf.at[pl.ds(pl.multiple_of((base + p) * tile, tile), tile)],
                insem.at[base + p],
            ).wait()
        for g in range(0, count_s, 2):
            at = pl.multiple_of((base + g) * tile, tile)
            for b in range(width // wide):
                gbuf[g // 2, b * wide:(b + 1) * wide, :] = lax.dot_general(
                    perm, xbuf[pl.ds(at, wide), b * wide:(b + 1) * wide], nt,
                    preferred_element_type=jnp.float32,
                ).astype(jnp.bfloat16)
                yield
            for b in range(width // wide):
                fitted = lax.dot_general(
                    gbuf[g // 2, b * wide:(b + 1) * wide, :], both[...], nt,
                    preferred_element_type=jnp.float32,
                ).astype(jnp.bfloat16)
                for t in range(2):
                    top = (g + t) * tile + b * span
                    for i in range(orbitals):
                        fbuf[top:top + span, i * tile:(i + 1) * tile] = fitted[
                            i * span:(i + 1) * span, t * tile:(t + 1) * tile
                        ]
                yield
        for g in range(0, count_s, 2):
            res[slot, g // 2, :(g + 2) * tile, :] = lax.dot_general(
                fbuf[:(g + 2) * tile, :], fbuf[g * tile:(g + 2) * tile, :], nt,
                preferred_element_type=jnp.float32,
            )
            yield

    def add(a, p, q):
        base = a * count_s
        slot = lax.rem(a, 2)
        first, second = ranked[base + p], ranked[base + q]
        d = first ^ second
        todo = []
        for h in range(2):
            jr = (second if h else first) ^ me
            unit = sz.chips if (h and p == q) else d
            entry = (jr * (sz.chips + 1) + unit) * 2
            for o in range(sz.cores):
                of_core = o ^ core
                row = pl.multiple_of(table_ref[entry + (of_core & 1)], sz.rows)
                where = pl.ds(row, sz.rows)
                at = pl.multiple_of(p * tile + h * half + of_core * sz.rows, sz.rows)
                new = res[
                    slot, q // 2, pl.ds(at, sz.rows), (q % 2) * tile:(q % 2 + 1) * tile
                ]
                old = send[o - 1, where, :] if o else keep[where, :]
                todo.append((o, where, old + new))
        for o, where, value in todo:
            if o:
                send[o - 1, where, :] = value
            else:
                keep[where, :] = value

    pairs = [(p, q) for p in range(count_s) for q in range(p, count_s)]

    def both_of(a, carry):
        left = list(pairs)
        for _ in tiles_of(a):
            if left:
                add(a - 1, *left.pop())
        while left:
            add(a - 1, *left.pop())
        return carry

    for _ in tiles_of(jnp.int32(0)):
        pass
    lax.fori_loop(1, count_a, both_of, 0)
    for p, q in pairs:
        add(jnp.int32(count_a - 1), p, q)


def place_kernel(sz, owner_ref, *refs):
    out, tiles = refs[-2], refs[-1]
    refs = refs[:-2]
    me = lax.axis_index("aux")
    core = lax.axis_index("occ")
    tile = out.shape[0]
    half = tile // 2
    n_plane = sz.count["plane"]
    for o in range(sz.cores):
        own, far = refs[2 * o:2 * o + 2]
        shift = (o ^ core) * sz.rows
        parity = (o ^ core) & 1
        for d in range(sz.chips):
            dp, dz = d % PLANE, d // PLANE
            p, q = [
                jnp.where(parity == 0, sz.place(x, bits, 0), sz.place(x, bits, 1))
                for x, bits in ((dp, 2), (dz, sz.bits - 2))
            ]
            if dp == 0:
                mine = own[n_plane + 1 + q]
            elif dz == 0:
                mine = own[p - 1]
            else:
                mine = far[(p - 1) * sz.lines + q]
            if d == 0:
                other = own[n_plane]
            elif dz == 0:
                other = far[(p - 1) * sz.lines]
            else:
                other = far[n_plane * sz.lines + (q - 1) * PLANE + p]
            top = (me >> (d.bit_length() - 1)) & 1 if d else 0
            tiles[d, pl.ds(pl.multiple_of(top * half + shift, sz.rows), sz.rows), :] = mine
            tiles[d, pl.ds(pl.multiple_of((1 - top) * half + shift, sz.rows), sz.rows), :] = other
    blocks = sz.chips // sz.cores
    for i in range(blocks):
        k = owner_ref[core * blocks + i]
        d = k ^ me

        @pl.when(me <= k)
        def _():
            out[:, i * tile:(i + 1) * tile] = tiles[d]

        @pl.when(me > k)
        def _():
            out[:, i * tile:(i + 1) * tile] = tiles[d].T


def local(three_index, fit_factor, slots, owner):
    _, count_a, count_s, tile, width = three_index.shape
    chips, cores = lax.axis_size("aux"), lax.axis_size("occ")
    sz = Sizes(chips, cores, tile)
    lines, rows = sz.lines, sz.rows
    f32 = jnp.float32

    def go(x, chip=0, core=0):
        if chip:
            return lax.ppermute(x, "aux", [(j, j ^ chip) for j in range(chips)])
        return lax.ppermute(x, "occ", [(j, j ^ core) for j in range(cores)])

    vmem = pl.BlockSpec(memory_space=pltpu.VMEM)
    smem = pl.BlockSpec(memory_space=pltpu.SMEM)
    hbm = pl.BlockSpec(memory_space=pltpu.HBM)
    small = 4 * cores * sz.total * tile < 2**24
    space = pltpu.VMEM if small else jax.ShapeDtypeStruct
    keep, send = pl.pallas_call(
        functools.partial(pair_kernel, sz),
        out_shape=[
            space((sz.total, tile), f32), space((cores - 1, sz.total, tile), f32),
        ],
        in_specs=[hbm] * 5,
        out_specs=[vmem, vmem],
        scratch_shapes=[
            pltpu.VMEM((count_a * count_s * tile, width), jnp.bfloat16),
            pltpu.VMEM((2 * tile, 2 * tile), jnp.bfloat16),
            pltpu.VMEM((count_s // 2, width, 2 * tile), jnp.bfloat16),
            pltpu.VMEM((count_s * tile, width), jnp.bfloat16),
            pltpu.VMEM((2, count_s // 2, count_s * tile, 2 * tile), f32),
            pltpu.VMEM(fit_factor.shape, jnp.bfloat16),
            pltpu.SMEM(slots.shape, jnp.int32),
            pltpu.SMEM(owner.shape, jnp.int32),
            pltpu.SMEM((chips * (chips + 1) * 2,), jnp.int32),
            pltpu.SMEM((count_a * count_s,), jnp.int32),
            pltpu.SemaphoreType.DMA((count_a * count_s,)),
            pltpu.SemaphoreType.DMA((4,)),
        ],
        compiler_params=pltpu.CompilerParams(
            vmem_limit_bytes=40 * 2**20 if small else 58 * 2**20
        ),
        name="pairs",
    )(*[
        pltpu.with_memory_space_constraint(x, pltpu.HBM)
        for x in (slots, owner, jnp.asarray(sz.table()), three_index, fit_factor)
    ])

    first = sz.at["cross", "s"][1]
    cuts = [(0, first), (first, sz.sent), (sz.sent, sz.total)]
    got = []
    for lo, hi in cuts:
        moved = []
        for e in range(1, cores):
            x = send[e - 1, lo:hi]
            if got:
                x = x + 0 * got[0][e - 1][:1]
            moved.append(go(x, core=e))
        got.append(moved)

    def step(x, name, k):
        pairs = []
        for j in range(chips):
            for c in range(cores):
                pairs.append((j * cores + c, (j ^ (1 << sz.order(name, c)[k])) * cores + c))
        return lax.ppermute(x, ("aux", "occ"), pairs)

    def total(terms):
        return functools.reduce(lambda a, b: a + b, terms)

    def terms(name, half):
        lo, hi = sz.at[name, half]
        shape = (chips // 2, sz.count[name], rows, tile)
        cut = 2 if half == "k" else int(name != "cross")
        off = cuts[cut][0]
        return [x.reshape(shape) for x in [keep[lo:hi]] + [g[lo - off:hi - off] for g in got[cut]]]

    parts, before = {}, None
    for k in range(sz.bits):
        for name in ("cross", "line", "plane"):
            if k:
                n = parts[name][0].shape[0] // 2
                sent, parts[name] = [x[n:] for x in parts[name]], [x[:n] for x in parts[name]]
            else:
                sent, parts[name] = terms(name, "s"), terms(name, "k")
            sent = total(sent)
            if before is not None:
                sent = sent + 0 * before[:sent.shape[0], :1]
            before = sent
            come = step(sent, name, k)
            parts[name].append(come)
    cross = total(parts["cross"])[0]
    line = total(parts["line"])[0] + 0 * cross[:1]
    plane = total(parts["plane"])[0] + 0 * line[:1]
    cross = cross.reshape(PLANE - 1, lines - 1, rows, tile)
    def across(blocks, name):
        for k in range(len(blocks).bit_length() - 1):
            moved = [q for q in range(len(blocks)) if q >> k & 1]
            come = step(jnp.stack([blocks[q] for q in moved]), name, k)
            for i, q in enumerate(moved):
                blocks[q] = come[i]
        return blocks[1:]

    far = [jnp.concatenate([line[1 + q:2 + q], cross[:, q - 1]]) for q in range(1, lines)]
    near = [jnp.concatenate([plane[q - 1:q], cross[q - 1]]) for q in range(1, PLANE)]
    far, near = across([None] + far, "line"), across([None] + near, "plane")
    own = jnp.concatenate([plane, line])
    far = jnp.concatenate(near + far)
    every = [own, far]
    for e in range(1, cores):
        every += [go(own, core=e), go(far, core=e)]

    result = pl.pallas_call(
        functools.partial(place_kernel, sz),
        out_shape=jax.ShapeDtypeStruct((tile, chips // cores * tile), f32),
        in_specs=[smem] + [vmem] * len(every),
        out_specs=vmem,
        scratch_shapes=[pltpu.VMEM((chips, tile, tile), f32)],
        compiler_params=pltpu.CompilerParams(vmem_limit_bytes=24 * 2**20),
        name="place",
    )(owner, *every)
    return result[None]


def solution(mesh):
    placed = (P("occ", "aux", None, None, None), P("aux", None, None), P("occ", "aux", None), P())
    return jax.shard_map(
        local, mesh=mesh, in_specs=placed, out_specs=P("aux", None, "occ"), check_vma=False
    )
```

```python
import functools

import jax
import jax.numpy as jnp
import numpy as np
from jax import lax
from jax.experimental import pallas as pl
from jax.experimental.pallas import tpu as pltpu
from jax.sharding import PartitionSpec as P

PLANE = 4


class Sizes:
    def __init__(self, chips, cores, tile):
        self.chips, self.cores = chips, cores
        self.lines = chips // PLANE
        self.rows = tile // 2 // cores
        self.bits = chips.bit_length() - 1
        self.count = {
            "cross": (PLANE - 1) * (self.lines - 1), "plane": PLANE - 1, "line": self.lines + 1,
        }
        self.at, total = {}, 0
        for half in ("s", "k"):
            for name, n in self.count.items():
                size = chips // 2 * n * self.rows
                self.at[name, half] = (total, total + size)
                total += size
        self.sent, self.total = total // 2, total

    def order(self, name, core):
        low, high = [0, 1], list(range(2, self.bits))
        if core % 2:
            low, high = low[::-1], high[::-1]
        return high + low if name == "line" else low + high

    def place(self, d, bits, parity):
        if parity and d >= 0:
            return sum((d >> b & 1) << (bits - 1 - b) for b in range(bits))
        return d

    def table(self):
        out = np.zeros((self.chips, self.chips + 1, 2), np.int32)
        for j in range(self.chips):
            for unit in range(self.chips + 1):
                dz, dp = (unit // PLANE, unit % PLANE) if unit < self.chips else (-1, 0)
                for parity in range(2):
                    p, q = self.place(dp, 2, parity), self.place(dz, self.bits - 2, parity)
                    if dp == 0:
                        name, i = "line", 1 + q
                    elif dz == 0:
                        name, i = "plane", p - 1
                    else:
                        name, i = "cross", (p - 1) * (self.lines - 1) + q - 1
                    row = 0
                    at = j ^ dp if name == "cross" else j
                    for bit in self.order(name, parity):
                        row = 2 * row + (at >> bit & 1)
                    half = self.chips // 2
                    base = self.at[name, "s" if row >= half else "k"][0]
                    row = (row % half) * self.count[name] + i
                    out[j, unit, parity] = base + row * self.rows
        return out.reshape(-1)


def pair_kernel(
    sz, slots_hbm, owner_hbm, table_hbm, x_ref, fit_hbm, keep, send,
    xbuf, both, gbuf, fbuf, res, fit_ref, slots_ref, owner_ref, table_ref, ranked, slot_of, insem, smallsem,
):
    _, count_a, count_s, tile, width = x_ref.shape
    orbitals = width // tile
    me = lax.axis_index("aux")
    core = lax.axis_index("occ")
    half = tile // 2
    small = [
        pltpu.make_async_copy(a, b, smallsem.at[i]) for i, (a, b) in enumerate([
            (slots_hbm, slots_ref), (owner_hbm, owner_ref), (fit_hbm, fit_ref),
            (table_hbm, table_ref),
        ])
    ]
    for c in small[:2]:
        c.start()

    def tile_copy(a, p):
        at = (a * count_s + p) * tile
        if not isinstance(a, int):
            at = pl.multiple_of(at, tile)
        return pltpu.make_async_copy(
            x_ref.at[0, a, p], xbuf.at[pl.ds(at, tile)], insem.at[a * count_s + p]
        )

    for p in range(count_s):
        tile_copy(0, p).start()
    small[2].start()
    small[3].start()
    keep[...] = jnp.zeros_like(keep)
    send[...] = jnp.zeros_like(send)
    both[...] = jnp.zeros_like(both)
    small[0].wait()
    small[1].wait()
    for a in range(count_a):
        own = [owner_ref[slots_ref[0, a, s]] for s in range(count_s)]
        for s in range(count_s):
            rank = jnp.int32(0)
            for t in range(count_s):
                if t != s:
                    rank = rank + (own[t] < own[s]).astype(jnp.int32)
            ranked[a * count_s + rank] = own[s]
            slot_of[a * count_s + rank] = s
    wide = 2 * tile
    span = wide // orbitals
    to = lax.broadcasted_iota(jnp.int32, (wide, wide), 0)
    of = lax.broadcasted_iota(jnp.int32, (wide, wide), 1)
    perm = (of == (to % span) * orbitals + to // span).astype(jnp.float32).astype(jnp.bfloat16)
    nt = (((1,), (1,)), ((), ()))
    small[2].wait()
    small[3].wait()

    def tiles_of(a):
        base = a * count_s
        slot = lax.rem(a, 2)
        both[:tile, :tile] = fit_ref[a]
        both[tile:, tile:] = fit_ref[a]
        for p in range(count_s):
            tile_copy(a, p).wait()
        for g in range(0, count_s, 2):
            rows = [
                pl.ds(pl.multiple_of((base + slot_of[base + g + t]) * tile, tile), tile)
                for t in range(2)
            ]
            for b in range(width // wide):
                two = [xbuf[r, b * wide:(b + 1) * wide] for r in rows]
                gbuf[g // 2, b * wide:(b + 1) * wide, :] = lax.dot_general(
                    perm, jnp.concatenate(two), nt,
                    preferred_element_type=jnp.float32,
                ).astype(jnp.bfloat16)
                yield
            for b in range(width // wide):
                fitted = lax.dot_general(
                    gbuf[g // 2, b * wide:(b + 1) * wide, :], both[...], nt,
                    preferred_element_type=jnp.float32,
                ).astype(jnp.bfloat16)
                for t in range(2):
                    top = (g + t) * tile + b * span
                    for i in range(orbitals):
                        fbuf[top:top + span, i * tile:(i + 1) * tile] = fitted[
                            i * span:(i + 1) * span, t * tile:(t + 1) * tile
                        ]
                yield
        for g in range(0, count_s, 2):
            res[slot, g // 2, :(g + 2) * tile, :] = lax.dot_general(
                fbuf[:(g + 2) * tile, :], fbuf[g * tile:(g + 2) * tile, :], nt,
                preferred_element_type=jnp.float32,
            )
            yield

    def add(a, p, q):
        base = a * count_s
        slot = lax.rem(a, 2)
        first, second = ranked[base + p], ranked[base + q]
        d = first ^ second
        todo = []
        for h in range(2):
            jr = (second if h else first) ^ me
            unit = sz.chips if (h and p == q) else d
            entry = (jr * (sz.chips + 1) + unit) * 2
            for o in range(sz.cores):
                of_core = o ^ core
                row = pl.multiple_of(table_ref[entry + (of_core & 1)], sz.rows)
                where = pl.ds(row, sz.rows)
                at = pl.multiple_of(p * tile + h * half + of_core * sz.rows, sz.rows)
                new = res[
                    slot, q // 2, pl.ds(at, sz.rows), (q % 2) * tile:(q % 2 + 1) * tile
                ]
                old = send[o - 1, where, :] if o else keep[where, :]
                todo.append((o, where, old + new))
        for o, where, value in todo:
            if o:
                send[o - 1, where, :] = value
            else:
                keep[where, :] = value

    pairs = [(p, q) for p in range(count_s) for q in range(p, count_s)]

    def both_of(a, carry):
        left = list(pairs)
        for _ in tiles_of(a):
            if left:
                add(a - 1, *left.pop())
        while left:
            add(a - 1, *left.pop())
        return carry

    for i, _ in enumerate(tiles_of(jnp.int32(0))):
        if i in (0, 8):
            for a in range(1, 2) if i == 0 else range(2, count_a):
                for p in range(count_s):
                    tile_copy(a, p).start()
    lax.fori_loop(1, count_a, both_of, 0)
    for p, q in pairs:
        add(jnp.int32(count_a - 1), p, q)


def place_kernel(sz, owner_ref, *refs):
    out, tiles = refs[-2], refs[-1]
    refs = refs[:-2]
    me = lax.axis_index("aux")
    core = lax.axis_index("occ")
    tile = out.shape[0]
    half = tile // 2
    n_plane = sz.count["plane"]
    for o in range(sz.cores):
        own, far = refs[2 * o:2 * o + 2]
        shift = (o ^ core) * sz.rows
        parity = (o ^ core) & 1
        for d in range(sz.chips):
            dp, dz = d % PLANE, d // PLANE
            p, q = [
                jnp.where(parity == 0, sz.place(x, bits, 0), sz.place(x, bits, 1))
                for x, bits in ((dp, 2), (dz, sz.bits - 2))
            ]
            if dp == 0:
                mine = own[n_plane + 1 + q]
            elif dz == 0:
                mine = own[p - 1]
            else:
                mine = far[(p - 1) * sz.lines + q]
            if d == 0:
                other = own[n_plane]
            elif dz == 0:
                other = far[(p - 1) * sz.lines]
            else:
                other = far[n_plane * sz.lines + (q - 1) * PLANE + p]
            top = (me >> (d.bit_length() - 1)) & 1 if d else 0
            tiles[d, pl.ds(pl.multiple_of(top * half + shift, sz.rows), sz.rows), :] = mine
            tiles[d, pl.ds(pl.multiple_of((1 - top) * half + shift, sz.rows), sz.rows), :] = other
    blocks = sz.chips // sz.cores
    for i in range(blocks):
        k = owner_ref[core * blocks + i]
        d = k ^ me

        @pl.when(me <= k)
        def _():
            out[:, i * tile:(i + 1) * tile] = tiles[d]

        @pl.when(me > k)
        def _():
            out[:, i * tile:(i + 1) * tile] = tiles[d].T


def local(three_index, fit_factor, slots, owner):
    _, count_a, count_s, tile, width = three_index.shape
    chips, cores = lax.axis_size("aux"), lax.axis_size("occ")
    sz = Sizes(chips, cores, tile)
    lines, rows = sz.lines, sz.rows
    f32 = jnp.float32

    def go(x, chip=0, core=0):
        if chip:
            return lax.ppermute(x, "aux", [(j, j ^ chip) for j in range(chips)])
        return lax.ppermute(x, "occ", [(j, j ^ core) for j in range(cores)])

    vmem = pl.BlockSpec(memory_space=pltpu.VMEM)
    smem = pl.BlockSpec(memory_space=pltpu.SMEM)
    hbm = pl.BlockSpec(memory_space=pltpu.HBM)
    small = 4 * cores * sz.total * tile < 2**24
    space = pltpu.VMEM if small else jax.ShapeDtypeStruct
    keep, send = pl.pallas_call(
        functools.partial(pair_kernel, sz),
        out_shape=[
            space((sz.total, tile), f32), space((cores - 1, sz.total, tile), f32),
        ],
        in_specs=[hbm] * 5,
        out_specs=[vmem, vmem],
        scratch_shapes=[
            pltpu.VMEM((count_a * count_s * tile, width), jnp.bfloat16),
            pltpu.VMEM((2 * tile, 2 * tile), jnp.bfloat16),
            pltpu.VMEM((count_s // 2, width, 2 * tile), jnp.bfloat16),
            pltpu.VMEM((count_s * tile, width), jnp.bfloat16),
            pltpu.VMEM((2, count_s // 2, count_s * tile, 2 * tile), f32),
            pltpu.VMEM(fit_factor.shape, jnp.bfloat16),
            pltpu.SMEM(slots.shape, jnp.int32),
            pltpu.SMEM(owner.shape, jnp.int32),
            pltpu.SMEM((chips * (chips + 1) * 2,), jnp.int32),
            pltpu.SMEM((count_a * count_s,), jnp.int32),
            pltpu.SMEM((count_a * count_s,), jnp.int32),
            pltpu.SemaphoreType.DMA((count_a * count_s,)),
            pltpu.SemaphoreType.DMA((4,)),
        ],
        compiler_params=pltpu.CompilerParams(
            vmem_limit_bytes=40 * 2**20 if small else 58 * 2**20
        ),
        name="pairs",
    )(*[
        pltpu.with_memory_space_constraint(x, pltpu.HBM)
        for x in (slots, owner, jnp.asarray(sz.table()), three_index, fit_factor)
    ])

    first = sz.at["cross", "s"][1]
    cuts = [(0, first), (first, sz.sent), (sz.sent, sz.total)]
    got = []
    for lo, hi in cuts:
        moved = []
        for e in range(1, cores):
            x = send[e - 1, lo:hi]
            if got:
                x = x + 0 * got[0][e - 1][:1]
            moved.append(go(x, core=e))
        got.append(moved)

    def step(x, name, k):
        pairs = []
        for j in range(chips):
            for c in range(cores):
                pairs.append((j * cores + c, (j ^ (1 << sz.order(name, c)[k])) * cores + c))
        return lax.ppermute(x, ("aux", "occ"), pairs)

    def total(terms):
        return functools.reduce(lambda a, b: a + b, terms)

    def terms(name, half):
        lo, hi = sz.at[name, half]
        shape = (chips // 2, sz.count[name], rows, tile)
        cut = 2 if half == "k" else int(name != "cross")
        off = cuts[cut][0]
        return [x.reshape(shape) for x in [keep[lo:hi]] + [g[lo - off:hi - off] for g in got[cut]]]

    parts, before = {}, None
    for k in range(sz.bits):
        for name in ("cross", "line", "plane"):
            if k:
                n = parts[name][0].shape[0] // 2
                sent, parts[name] = [x[n:] for x in parts[name]], [x[:n] for x in parts[name]]
            else:
                sent, parts[name] = terms(name, "s"), terms(name, "k")
            sent = total(sent)
            if before is not None:
                sent = sent + 0 * before[:sent.shape[0], :1]
            before = sent
            come = step(sent, name, k)
            parts[name].append(come)
    cross = total(parts["cross"])[0]
    line = total(parts["line"])[0] + 0 * cross[:1]
    plane = total(parts["plane"])[0] + 0 * line[:1]
    cross = cross.reshape(PLANE - 1, lines - 1, rows, tile)
    def across(blocks, name):
        for k in range(len(blocks).bit_length() - 1):
            moved = [q for q in range(len(blocks)) if q >> k & 1]
            come = step(jnp.stack([blocks[q] for q in moved]), name, k)
            for i, q in enumerate(moved):
                blocks[q] = come[i]
        return blocks[1:]

    far = [jnp.concatenate([line[1 + q:2 + q], cross[:, q - 1]]) for q in range(1, lines)]
    near = [jnp.concatenate([plane[q - 1:q], cross[q - 1]]) for q in range(1, PLANE)]
    far, near = across([None] + far, "line"), across([None] + near, "plane")
    own = jnp.concatenate([plane, line])
    far = jnp.concatenate(near + far)
    every = [own, far]
    for e in range(1, cores):
        every += [go(own, core=e), go(far, core=e)]

    result = pl.pallas_call(
        functools.partial(place_kernel, sz),
        out_shape=jax.ShapeDtypeStruct((tile, chips // cores * tile), f32),
        in_specs=[smem] + [vmem] * len(every),
        out_specs=vmem,
        scratch_shapes=[pltpu.VMEM((chips, tile, tile), f32)],
        compiler_params=pltpu.CompilerParams(vmem_limit_bytes=24 * 2**20),
        name="place",
    )(owner, *every)
    return result[None]


def solution(mesh):
    placed = (P("occ", "aux", None, None, None), P("aux", None, None), P("occ", "aux", None), P())
    return jax.shard_map(
        local, mesh=mesh, in_specs=placed, out_specs=P("aux", None, "occ"), check_vma=False
    )
```

```python
import functools

import jax
import jax.numpy as jnp
import numpy as np
from jax import lax
from jax.experimental import pallas as pl
from jax.experimental.pallas import tpu as pltpu
from jax.sharding import PartitionSpec as P

PLANE = 4


class Sizes:
    def __init__(self, chips, cores, tile):
        self.chips, self.cores = chips, cores
        self.lines = chips // PLANE
        self.rows = tile // 2 // cores
        self.bits = chips.bit_length() - 1
        self.pack = self.rows // 2 if self.rows >= 16 else self.rows
        self.size = {
            "cross": (PLANE - 1) * (self.lines - 1) * self.rows,
            "plane": (PLANE - 1) * self.rows + self.pack, "line": self.lines * self.rows,
        }
        self.at, total = {}, 0
        for half in ("s", "k"):
            for name, n in self.size.items():
                size = chips // 2 * n
                self.at[name, half] = (total, total + size)
                total += size
        self.sent, self.total = total // 2, total

    def order(self, name, core):
        low, high = [0, 1], list(range(2, self.bits))
        if core % 2:
            low, high = low[::-1], high[::-1]
        return high + low if name == "line" else low + high

    def place(self, d, bits, parity):
        if parity and d >= 0:
            return sum((d >> b & 1) << (bits - 1 - b) for b in range(bits))
        return d

    def table(self):
        out = np.zeros((self.chips, self.chips + 1, 2), np.int32)
        for j in range(self.chips):
            for unit in range(self.chips + 1):
                dz, dp = (unit // PLANE, unit % PLANE) if unit < self.chips else (-1, 0)
                for parity in range(2):
                    p, q = self.place(dp, 2, parity), self.place(dz, self.bits - 2, parity)
                    if dz < 0:
                        name, i = "plane", (PLANE - 1) * self.rows
                    elif dp == 0:
                        name, i = "line", q * self.rows
                    elif dz == 0:
                        name, i = "plane", (p - 1) * self.rows
                    else:
                        name, i = "cross", ((p - 1) * (self.lines - 1) + q - 1) * self.rows
                    row = 0
                    at = j ^ dp if name == "cross" else j
                    for bit in self.order(name, parity):
                        row = 2 * row + (at >> bit & 1)
                    half = self.chips // 2
                    base = self.at[name, "s" if row >= half else "k"][0]
                    out[j, unit, parity] = base + (row % half) * self.size[name] + i
        return out.reshape(-1)


def pair_kernel(
    sz, slots_hbm, owner_hbm, table_hbm, x_ref, fit_hbm, keep, send,
    xbuf, both, gbuf, fbuf, res, fit_ref, slots_ref, owner_ref, table_ref, ranked, slot_of, insem, smallsem,
):
    _, count_a, count_s, tile, width = x_ref.shape
    orbitals = width // tile
    me = lax.axis_index("aux")
    core = lax.axis_index("occ")
    half = tile // 2
    small = [
        pltpu.make_async_copy(a, b, smallsem.at[i]) for i, (a, b) in enumerate([
            (slots_hbm, slots_ref), (owner_hbm, owner_ref), (fit_hbm, fit_ref),
            (table_hbm, table_ref),
        ])
    ]
    for c in small[:2]:
        c.start()

    def tile_copy(a, p):
        at = (a * count_s + p) * tile
        if not isinstance(a, int):
            at = pl.multiple_of(at, tile)
        return pltpu.make_async_copy(
            x_ref.at[0, a, p], xbuf.at[pl.ds(at, tile)], insem.at[a * count_s + p]
        )

    for p in range(count_s):
        tile_copy(0, p).start()
    small[2].start()
    small[3].start()
    keep[...] = jnp.zeros_like(keep)
    send[...] = jnp.zeros_like(send)
    both[...] = jnp.zeros_like(both)
    small[0].wait()
    small[1].wait()
    for a in range(count_a):
        own = [owner_ref[slots_ref[0, a, s]] for s in range(count_s)]
        for s in range(count_s):
            rank = jnp.int32(0)
            for t in range(count_s):
                if t != s:
                    rank = rank + (own[t] < own[s]).astype(jnp.int32)
            ranked[a * count_s + rank] = own[s]
            slot_of[a * count_s + rank] = s
    wide = 2 * tile
    span = wide // orbitals
    to = lax.broadcasted_iota(jnp.int32, (wide, wide), 0)
    of = lax.broadcasted_iota(jnp.int32, (wide, wide), 1)
    perm = (of == (to % span) * orbitals + to // span).astype(jnp.float32).astype(jnp.bfloat16)
    nt = (((1,), (1,)), ((), ()))
    small[2].wait()
    small[3].wait()

    def tiles_of(a):
        base = a * count_s
        slot = lax.rem(a, 2)
        both[:tile, :tile] = fit_ref[a]
        both[tile:, tile:] = fit_ref[a]
        for p in range(count_s):
            tile_copy(a, p).wait()
        for g in range(0, count_s, 2):
            rows = [
                pl.ds(pl.multiple_of((base + slot_of[base + g + t]) * tile, tile), tile)
                for t in range(2)
            ]
            for b in range(width // wide):
                two = [xbuf[r, b * wide:(b + 1) * wide] for r in rows]
                gbuf[g // 2, b * wide:(b + 1) * wide, :] = lax.dot_general(
                    perm, jnp.concatenate(two), nt,
                    preferred_element_type=jnp.float32,
                ).astype(jnp.bfloat16)
                yield
            for b in range(width // wide):
                fitted = lax.dot_general(
                    gbuf[g // 2, b * wide:(b + 1) * wide, :], both[...], nt,
                    preferred_element_type=jnp.float32,
                ).astype(jnp.bfloat16)
                for t in range(2):
                    top = (g + t) * tile + b * span
                    for i in range(orbitals):
                        fbuf[top:top + span, i * tile:(i + 1) * tile] = fitted[
                            i * span:(i + 1) * span, t * tile:(t + 1) * tile
                        ]
                yield
        for g in range(0, count_s, 2):
            res[slot, g // 2, :(g + 2) * tile, :] = lax.dot_general(
                fbuf[:(g + 2) * tile, :], fbuf[g * tile:(g + 2) * tile, :], nt,
                preferred_element_type=jnp.float32,
            )
            yield

    def add(a, p, q):
        base = a * count_s
        slot = lax.rem(a, 2)
        first, second = ranked[base + p], ranked[base + q]
        d = first ^ second
        todo = []
        for h in range(2):
            jr = (second if h else first) ^ me
            unit = sz.chips if (h and p == q) else d
            entry = (jr * (sz.chips + 1) + unit) * 2
            for o in range(sz.cores):
                of_core = o ^ core
                row = pl.multiple_of(table_ref[entry + (of_core & 1)], sz.pack)
                where = pl.ds(row, sz.rows)
                at = pl.multiple_of(p * tile + h * half + of_core * sz.rows, sz.rows)
                new = res[
                    slot, q // 2, pl.ds(at, sz.rows), (q % 2) * tile:(q % 2 + 1) * tile
                ]
                if h and p == q and sz.pack < sz.rows:
                    where = pl.ds(row, sz.pack)
                    lane = lax.broadcasted_iota(jnp.int32, (sz.pack, tile), 1)
                    new = jnp.where(
                        lane < half, pltpu.roll(new[:sz.pack], half, 1), new[sz.pack:]
                    )
                old = send[o - 1, where, :] if o else keep[where, :]
                todo.append((o, where, old + new))
        for o, where, value in todo:
            if o:
                send[o - 1, where, :] = value
            else:
                keep[where, :] = value

    pairs = [(p, q) for p in range(count_s) for q in range(p, count_s)]

    def both_of(a, carry):
        left = list(pairs)
        for _ in tiles_of(a):
            if left:
                add(a - 1, *left.pop())
        while left:
            add(a - 1, *left.pop())
        return carry

    for i, _ in enumerate(tiles_of(jnp.int32(0))):
        if i in (0, 8):
            for a in range(1, 2) if i == 0 else range(2, count_a):
                for p in range(count_s):
                    tile_copy(a, p).start()
    lax.fori_loop(1, count_a, both_of, 0)
    for p, q in pairs:
        add(jnp.int32(count_a - 1), p, q)


def place_kernel(sz, owner_ref, *refs):
    out, tiles = refs[-2], refs[-1]
    refs = refs[:-2]
    me = lax.axis_index("aux")
    core = lax.axis_index("occ")
    tile = out.shape[0]
    half = tile // 2
    n_plane = PLANE - 1
    line_at = n_plane * sz.rows + sz.pack
    for o in range(sz.cores):
        own, far = refs[2 * o:2 * o + 2]
        shift = (o ^ core) * sz.rows
        parity = (o ^ core) & 1
        for d in range(sz.chips):
            dp, dz = d % PLANE, d // PLANE
            p, q = [
                jnp.where(parity == 0, sz.place(x, bits, 0), sz.place(x, bits, 1))
                for x, bits in ((dp, 2), (dz, sz.bits - 2))
            ]
            if dp == 0:
                mine = own[pl.ds(pl.multiple_of(line_at + q * sz.rows, sz.pack), sz.rows)]
            elif dz == 0:
                mine = own[pl.ds(pl.multiple_of((p - 1) * sz.rows, sz.rows), sz.rows)]
            else:
                mine = far[(p - 1) * sz.lines + q]
            if d == 0:
                other = own[line_at - sz.pack:line_at]
                if sz.pack < sz.rows:
                    other = jnp.concatenate([pltpu.roll(other, half, 1), other])
            elif dz == 0:
                other = far[(p - 1) * sz.lines]
            else:
                other = far[n_plane * sz.lines + (q - 1) * PLANE + p]
            top = (me >> (d.bit_length() - 1)) & 1 if d else 0
            tiles[d, pl.ds(pl.multiple_of(top * half + shift, sz.rows), sz.rows), :] = mine
            tiles[d, pl.ds(pl.multiple_of((1 - top) * half + shift, sz.rows), sz.rows), :] = other
    if sz.pack < sz.rows:
        row = lax.broadcasted_iota(jnp.int32, (tile, tile), 0)
        column = lax.broadcasted_iota(jnp.int32, (tile, tile), 1)
        whole = tiles[0]
        tiles[0] = jnp.where((row >= half) & (column < half), whole.T, whole)
    blocks = sz.chips // sz.cores
    for i in range(blocks):
        k = owner_ref[core * blocks + i]
        d = k ^ me

        @pl.when(me <= k)
        def _():
            out[:, i * tile:(i + 1) * tile] = tiles[d]

        @pl.when(me > k)
        def _():
            out[:, i * tile:(i + 1) * tile] = tiles[d].T


def local(three_index, fit_factor, slots, owner):
    _, count_a, count_s, tile, width = three_index.shape
    chips, cores = lax.axis_size("aux"), lax.axis_size("occ")
    sz = Sizes(chips, cores, tile)
    lines, rows = sz.lines, sz.rows
    f32 = jnp.float32

    def go(x, chip=0, core=0):
        if chip:
            return lax.ppermute(x, "aux", [(j, j ^ chip) for j in range(chips)])
        return lax.ppermute(x, "occ", [(j, j ^ core) for j in range(cores)])

    vmem = pl.BlockSpec(memory_space=pltpu.VMEM)
    smem = pl.BlockSpec(memory_space=pltpu.SMEM)
    hbm = pl.BlockSpec(memory_space=pltpu.HBM)
    small = 4 * cores * sz.total * tile < 2**24
    space = pltpu.VMEM if small else jax.ShapeDtypeStruct
    keep, send = pl.pallas_call(
        functools.partial(pair_kernel, sz),
        out_shape=[
            space((sz.total, tile), f32), space((cores - 1, sz.total, tile), f32),
        ],
        in_specs=[hbm] * 5,
        out_specs=[vmem, vmem],
        scratch_shapes=[
            pltpu.VMEM((count_a * count_s * tile, width), jnp.bfloat16),
            pltpu.VMEM((2 * tile, 2 * tile), jnp.bfloat16),
            pltpu.VMEM((count_s // 2, width, 2 * tile), jnp.bfloat16),
            pltpu.VMEM((count_s * tile, width), jnp.bfloat16),
            pltpu.VMEM((2, count_s // 2, count_s * tile, 2 * tile), f32),
            pltpu.VMEM(fit_factor.shape, jnp.bfloat16),
            pltpu.SMEM(slots.shape, jnp.int32),
            pltpu.SMEM(owner.shape, jnp.int32),
            pltpu.SMEM((chips * (chips + 1) * 2,), jnp.int32),
            pltpu.SMEM((count_a * count_s,), jnp.int32),
            pltpu.SMEM((count_a * count_s,), jnp.int32),
            pltpu.SemaphoreType.DMA((count_a * count_s,)),
            pltpu.SemaphoreType.DMA((4,)),
        ],
        compiler_params=pltpu.CompilerParams(
            vmem_limit_bytes=40 * 2**20 if small else 58 * 2**20
        ),
        name="pairs",
    )(*[
        pltpu.with_memory_space_constraint(x, pltpu.HBM)
        for x in (slots, owner, jnp.asarray(sz.table()), three_index, fit_factor)
    ])

    first = sz.at["cross", "s"][1]
    cuts = [(0, first), (first, sz.sent), (sz.sent, sz.total)]
    got = []
    for lo, hi in cuts:
        moved = []
        for e in range(1, cores):
            x = send[e - 1, lo:hi]
            if got:
                x = x + 0 * got[0][e - 1][:1]
            moved.append(go(x, core=e))
        got.append(moved)

    def step(x, name, k):
        pairs = []
        for j in range(chips):
            for c in range(cores):
                pairs.append((j * cores + c, (j ^ (1 << sz.order(name, c)[k])) * cores + c))
        return lax.ppermute(x, ("aux", "occ"), pairs)

    def total(terms):
        return functools.reduce(lambda a, b: a + b, terms)

    def terms(name, half):
        lo, hi = sz.at[name, half]
        shape = (chips // 2, sz.size[name], tile)
        cut = 2 if half == "k" else int(name != "cross")
        off = cuts[cut][0]
        return [x.reshape(shape) for x in [keep[lo:hi]] + [g[lo - off:hi - off] for g in got[cut]]]

    parts, before = {}, None
    for k in range(sz.bits):
        for name in ("cross", "line", "plane"):
            if k:
                n = parts[name][0].shape[0] // 2
                sent, parts[name] = [x[n:] for x in parts[name]], [x[:n] for x in parts[name]]
            else:
                sent, parts[name] = terms(name, "s"), terms(name, "k")
            sent = total(sent)
            if before is not None:
                sent = sent + 0 * before[:sent.shape[0], :1]
            before = sent
            come = step(sent, name, k)
            parts[name].append(come)
    cross = total(parts["cross"])[0]
    line = total(parts["line"])[0] + 0 * cross[:1]
    plane = total(parts["plane"])[0] + 0 * line[:1]
    own = jnp.concatenate([plane, line])
    cross = cross.reshape(PLANE - 1, lines - 1, rows, tile)
    plane, line = plane[:-sz.pack].reshape(-1, rows, tile), line.reshape(lines, rows, tile)
    def across(blocks, name):
        for k in range(len(blocks).bit_length() - 1):
            moved = [q for q in range(len(blocks)) if q >> k & 1]
            come = step(jnp.stack([blocks[q] for q in moved]), name, k)
            for i, q in enumerate(moved):
                blocks[q] = come[i]
        return blocks[1:]

    far = [jnp.concatenate([line[q:q + 1], cross[:, q - 1]]) for q in range(1, lines)]
    near = [jnp.concatenate([plane[q - 1:q], cross[q - 1]]) for q in range(1, PLANE)]
    far, near = across([None] + far, "line"), across([None] + near, "plane")
    far = jnp.concatenate(near + far)
    every = [own, far]
    for e in range(1, cores):
        every += [go(own, core=e), go(far, core=e)]

    result = pl.pallas_call(
        functools.partial(place_kernel, sz),
        out_shape=jax.ShapeDtypeStruct((tile, chips // cores * tile), f32),
        in_specs=[smem] + [vmem] * len(every),
        out_specs=vmem,
        scratch_shapes=[pltpu.VMEM((chips, tile, tile), f32)],
        compiler_params=pltpu.CompilerParams(vmem_limit_bytes=24 * 2**20),
        name="place",
    )(owner, *every)
    return result[None]


def solution(mesh):
    placed = (P("occ", "aux", None, None, None), P("aux", None, None), P("occ", "aux", None), P())
    return jax.shard_map(
        local, mesh=mesh, in_specs=placed, out_specs=P("aux", None, "occ"), check_vma=False
    )
```

```python
import functools

import jax
import jax.numpy as jnp
import numpy as np
from jax import lax
from jax.experimental import pallas as pl
from jax.experimental.pallas import tpu as pltpu
from jax.sharding import PartitionSpec as P

PLANE = 4


class Sizes:
    def __init__(self, chips, cores, tile):
        self.chips, self.cores = chips, cores
        self.lines = chips // PLANE
        self.rows = tile // 2 // cores
        self.bits = chips.bit_length() - 1
        self.pack = self.rows // 2 if self.rows >= 16 else self.rows
        self.size = {
            "cross": (PLANE - 1) * (self.lines - 1) * self.rows,
            "plane": (PLANE - 1) * self.rows + self.pack, "line": self.lines * self.rows,
        }
        self.at, total = {}, 0
        for half in ("s", "k"):
            for name, n in self.size.items():
                size = chips // 2 * n
                self.at[name, half] = (total, total + size)
                total += size
        self.sent, self.total = total // 2, total

    def order(self, name, core):
        low, high = [0, 1], list(range(2, self.bits))
        if core % 2:
            low, high = low[::-1], high[::-1]
        return high + low if name == "line" else low + high

    def place(self, d, bits, parity):
        if parity and d >= 0:
            return sum((d >> b & 1) << (bits - 1 - b) for b in range(bits))
        return d

    def table(self):
        out = np.zeros((self.chips, self.chips + 1, 2), np.int32)
        for j in range(self.chips):
            for unit in range(self.chips + 1):
                dz, dp = (unit // PLANE, unit % PLANE) if unit < self.chips else (-1, 0)
                for parity in range(2):
                    p, q = self.place(dp, 2, parity), self.place(dz, self.bits - 2, parity)
                    if dz < 0:
                        name, i = "plane", (PLANE - 1) * self.rows
                    elif dp == 0:
                        name, i = "line", q * self.rows
                    elif dz == 0:
                        name, i = "plane", (p - 1) * self.rows
                    else:
                        name, i = "cross", ((p - 1) * (self.lines - 1) + q - 1) * self.rows
                    row = 0
                    at = j ^ dp if name == "cross" else j
                    for bit in self.order(name, parity):
                        row = 2 * row + (at >> bit & 1)
                    half = self.chips // 2
                    base = self.at[name, "s" if row >= half else "k"][0]
                    out[j, unit, parity] = base + (row % half) * self.size[name] + i
        return out.reshape(-1)


def pair_kernel(
    sz, slots_hbm, owner_hbm, table_hbm, x_ref, fit_hbm, keep, send,
    xbuf, both, gbuf, fbuf, res, fit_ref, slots_ref, owner_ref, table_ref, ranked, slot_of, insem, smallsem,
):
    _, count_a, count_s, tile, width = x_ref.shape
    orbitals = width // tile
    me = lax.axis_index("aux")
    core = lax.axis_index("occ")
    half = tile // 2
    small = [
        pltpu.make_async_copy(a, b, smallsem.at[i]) for i, (a, b) in enumerate([
            (slots_hbm, slots_ref), (owner_hbm, owner_ref), (fit_hbm, fit_ref),
            (table_hbm, table_ref),
        ])
    ]
    for c in small[:2]:
        c.start()

    def tile_copy(a, p):
        at = (a * count_s + p) * tile
        if not isinstance(a, int):
            at = pl.multiple_of(at, tile)
        return pltpu.make_async_copy(
            x_ref.at[0, a, p], xbuf.at[pl.ds(at, tile)], insem.at[a * count_s + p]
        )

    for p in range(count_s):
        tile_copy(0, p).start()
    small[2].start()
    small[3].start()
    keep[...] = jnp.zeros_like(keep)
    send[...] = jnp.zeros_like(send)
    both[...] = jnp.zeros_like(both)
    small[0].wait()
    small[1].wait()
    for a in range(count_a):
        own = [owner_ref[slots_ref[0, a, s]] for s in range(count_s)]
        for s in range(count_s):
            rank = jnp.int32(0)
            for t in range(count_s):
                if t != s:
                    rank = rank + (own[t] < own[s]).astype(jnp.int32)
            ranked[a * count_s + rank] = own[s]
            slot_of[a * count_s + rank] = s
    wide = 2 * tile
    span = wide // orbitals
    to = lax.broadcasted_iota(jnp.int32, (wide, wide), 0)
    of = lax.broadcasted_iota(jnp.int32, (wide, wide), 1)
    perm = (of == (to % span) * orbitals + to // span).astype(jnp.float32).astype(jnp.bfloat16)
    nt = (((1,), (1,)), ((), ()))
    small[2].wait()
    small[3].wait()

    def tiles_of(a):
        base = a * count_s
        slot = lax.rem(a, 2)
        both[:tile, :tile] = fit_ref[a]
        both[tile:, tile:] = fit_ref[a]
        for p in range(count_s):
            tile_copy(a, p).wait()
        for g in range(0, count_s, 2):
            rows = [
                pl.ds(pl.multiple_of((base + slot_of[base + g + t]) * tile, tile), tile)
                for t in range(2)
            ]
            for b in range(width // wide):
                two = [xbuf[r, b * wide:(b + 1) * wide] for r in rows]
                gbuf[g // 2, b * wide:(b + 1) * wide, :] = lax.dot_general(
                    perm, jnp.concatenate(two), nt,
                    preferred_element_type=jnp.float32,
                ).astype(jnp.bfloat16)
                yield
            for b in range(width // wide):
                fitted = lax.dot_general(
                    gbuf[g // 2, b * wide:(b + 1) * wide, :], both[...], nt,
                    preferred_element_type=jnp.float32,
                ).astype(jnp.bfloat16)
                for t in range(2):
                    top = (g + t) * tile + b * span
                    for i in range(orbitals):
                        fbuf[top:top + span, i * tile:(i + 1) * tile] = fitted[
                            i * span:(i + 1) * span, t * tile:(t + 1) * tile
                        ]
                yield
        for g in range(0, count_s, 2):
            res[slot, g // 2, :(g + 2) * tile, :] = lax.dot_general(
                fbuf[:(g + 2) * tile, :], fbuf[g * tile:(g + 2) * tile, :], nt,
                preferred_element_type=jnp.float32,
            )
            yield

    def add(a, p, q):
        base = a * count_s
        slot = lax.rem(a, 2)
        first, second = ranked[base + p], ranked[base + q]
        d = first ^ second
        todo = []
        for h in range(2):
            jr = (second if h else first) ^ me
            unit = sz.chips if (h and p == q) else d
            entry = (jr * (sz.chips + 1) + unit) * 2
            for o in range(sz.cores):
                of_core = o ^ core
                row = pl.multiple_of(table_ref[entry + (of_core & 1)], sz.pack)
                where = pl.ds(row, sz.rows)
                at = pl.multiple_of(p * tile + h * half + of_core * sz.rows, sz.rows)
                new = res[
                    slot, q // 2, pl.ds(at, sz.rows), (q % 2) * tile:(q % 2 + 1) * tile
                ]
                if h and p == q and sz.pack < sz.rows:
                    where = pl.ds(row, sz.pack)
                    lane = lax.broadcasted_iota(jnp.int32, (sz.pack, tile), 1)
                    new = jnp.where(
                        lane < half, pltpu.roll(new[:sz.pack], half, 1), new[sz.pack:]
                    )
                old = send[o - 1, where, :] if o else keep[where, :]
                todo.append((o, where, old + new))
        for o, where, value in todo:
            if o:
                send[o - 1, where, :] = value
            else:
                keep[where, :] = value

    pairs = [(p, q) for p in range(count_s) for q in range(p, count_s)]

    def both_of(a, carry):
        left = list(pairs)
        for _ in tiles_of(a):
            if left:
                add(a - 1, *left.pop())
        while left:
            add(a - 1, *left.pop())
        return carry

    for i, _ in enumerate(tiles_of(jnp.int32(0))):
        if i in (0, 8):
            for a in range(1, 2) if i == 0 else range(2, count_a):
                for p in range(count_s):
                    tile_copy(a, p).start()
    lax.fori_loop(1, count_a, both_of, 0)
    for p, q in pairs:
        add(jnp.int32(count_a - 1), p, q)


def place_kernel(sz, owner_ref, *refs):
    out, tiles = refs[-2], refs[-1]
    refs = refs[:-2]
    me = lax.axis_index("aux")
    core = lax.axis_index("occ")
    tile = out.shape[0]
    half = tile // 2
    n_plane = PLANE - 1
    line_at = n_plane * sz.rows + sz.pack
    for o in range(sz.cores):
        own, far = refs[2 * o:2 * o + 2]
        shift = (o ^ core) * sz.rows
        parity = (o ^ core) & 1
        for d in range(sz.chips):
            dp, dz = d % PLANE, d // PLANE
            p, q = [
                jnp.where(parity == 0, sz.place(x, bits, 0), sz.place(x, bits, 1))
                for x, bits in ((dp, 2), (dz, sz.bits - 2))
            ]
            if dp == 0:
                mine = own[pl.ds(pl.multiple_of(line_at + q * sz.rows, sz.pack), sz.rows)]
            elif dz == 0:
                mine = own[pl.ds(pl.multiple_of((p - 1) * sz.rows, sz.rows), sz.rows)]
            else:
                mine = far[(p - 1) * sz.lines + q]
            if d == 0:
                other = own[line_at - sz.pack:line_at]
                if sz.pack < sz.rows:
                    other = jnp.concatenate([pltpu.roll(other, half, 1), other])
            elif dz == 0:
                other = far[(p - 1) * sz.lines]
            else:
                other = far[n_plane * sz.lines + (q - 1) * PLANE + p]
            top = (me >> (d.bit_length() - 1)) & 1 if d else 0
            tiles[d, pl.ds(pl.multiple_of(top * half + shift, sz.rows), sz.rows), :] = mine
            tiles[d, pl.ds(pl.multiple_of((1 - top) * half + shift, sz.rows), sz.rows), :] = other
    if sz.pack < sz.rows:
        row = lax.broadcasted_iota(jnp.int32, (tile, tile), 0)
        column = lax.broadcasted_iota(jnp.int32, (tile, tile), 1)
        whole = tiles[0]
        tiles[0] = jnp.where((row >= half) & (column < half), whole.T, whole)
    blocks = sz.chips // sz.cores
    for i in range(blocks):
        k = owner_ref[core * blocks + i]
        d = k ^ me

        @pl.when(me <= k)
        def _():
            out[:, i * tile:(i + 1) * tile] = tiles[d]

        @pl.when(me > k)
        def _():
            out[:, i * tile:(i + 1) * tile] = tiles[d].T


def local(three_index, fit_factor, slots, owner):
    _, count_a, count_s, tile, width = three_index.shape
    chips, cores = lax.axis_size("aux"), lax.axis_size("occ")
    sz = Sizes(chips, cores, tile)
    lines, rows = sz.lines, sz.rows
    f32 = jnp.float32

    def go(x, chip=0, core=0):
        if chip:
            return lax.ppermute(x, "aux", [(j, j ^ chip) for j in range(chips)])
        return lax.ppermute(x, "occ", [(j, j ^ core) for j in range(cores)])

    vmem = pl.BlockSpec(memory_space=pltpu.VMEM)
    smem = pl.BlockSpec(memory_space=pltpu.SMEM)
    hbm = pl.BlockSpec(memory_space=pltpu.HBM)
    small = 4 * cores * sz.total * tile < 2**24
    space = pltpu.VMEM if small else jax.ShapeDtypeStruct
    keep, send = pl.pallas_call(
        functools.partial(pair_kernel, sz),
        out_shape=[
            space((sz.total, tile), f32), space((cores - 1, sz.total, tile), f32),
        ],
        in_specs=[hbm] * 5,
        out_specs=[vmem, vmem],
        scratch_shapes=[
            pltpu.VMEM((count_a * count_s * tile, width), jnp.bfloat16),
            pltpu.VMEM((2 * tile, 2 * tile), jnp.bfloat16),
            pltpu.VMEM((count_s // 2, width, 2 * tile), jnp.bfloat16),
            pltpu.VMEM((count_s * tile, width), jnp.bfloat16),
            pltpu.VMEM((2, count_s // 2, count_s * tile, 2 * tile), f32),
            pltpu.VMEM(fit_factor.shape, jnp.bfloat16),
            pltpu.SMEM(slots.shape, jnp.int32),
            pltpu.SMEM(owner.shape, jnp.int32),
            pltpu.SMEM((chips * (chips + 1) * 2,), jnp.int32),
            pltpu.SMEM((count_a * count_s,), jnp.int32),
            pltpu.SMEM((count_a * count_s,), jnp.int32),
            pltpu.SemaphoreType.DMA((count_a * count_s,)),
            pltpu.SemaphoreType.DMA((4,)),
        ],
        compiler_params=pltpu.CompilerParams(
            vmem_limit_bytes=40 * 2**20 if small else 58 * 2**20
        ),
        name="pairs",
    )(*[
        pltpu.with_memory_space_constraint(x, pltpu.HBM)
        for x in (slots, owner, jnp.asarray(sz.table()), three_index, fit_factor)
    ])

    first = sz.at["cross", "s"][1]
    cuts = [(0, first), (first, sz.sent), (sz.sent, sz.total)]
    got = []
    for lo, hi in cuts:
        moved = []
        for e in range(1, cores):
            x = send[e - 1, lo:hi]
            if got:
                x = x + 0 * got[0][e - 1][:1]
            moved.append(go(x, core=e))
        got.append(moved)

    def step(x, name, k):
        pairs = []
        for j in range(chips):
            for c in range(cores):
                pairs.append((j * cores + c, (j ^ (1 << sz.order(name, c)[k])) * cores + c))
        return lax.ppermute(x, ("aux", "occ"), pairs)

    def total(terms):
        return functools.reduce(lambda a, b: a + b, terms)

    def terms(name, half):
        lo, hi = sz.at[name, half]
        shape = (chips // 2, sz.size[name], tile)
        cut = 2 if half == "k" else int(name != "cross")
        off = cuts[cut][0]
        return [x.reshape(shape) for x in [keep[lo:hi]] + [g[lo - off:hi - off] for g in got[cut]]]

    parts, before = {}, None
    for k in range(sz.bits):
        for name in ("cross", "line", "plane"):
            if k:
                n = parts[name][0].shape[0] // 2
                sent, parts[name] = [x[n:] for x in parts[name]], [x[:n] for x in parts[name]]
                if k == 1 and name == "line":
                    sent, parts[name] = sent + [upper], parts[name] + [lower]
            else:
                sent, parts[name] = terms(name, "s"), terms(name, "k")
            sent = total(sent)
            if before is not None:
                sent = sent + 0 * before[:sent.shape[0], :1]
            before = sent
            if k == 0 and name == "line":
                n = chips // 4
                upper, lower = step(sent[n:], name, k), step(sent[:n], name, k)
            else:
                parts[name].append(step(sent, name, k))
    cross = total(parts["cross"])[0]
    line = total(parts["line"])[0] + 0 * cross[:1]
    plane = total(parts["plane"])[0] + 0 * line[:1]
    own = jnp.concatenate([plane, line])
    cross = cross.reshape(PLANE - 1, lines - 1, rows, tile)
    plane, line = plane[:-sz.pack].reshape(-1, rows, tile), line.reshape(lines, rows, tile)
    def across(blocks, name):
        for k in range(len(blocks).bit_length() - 1):
            moved = [q for q in range(len(blocks)) if q >> k & 1]
            come = step(jnp.stack([blocks[q] for q in moved]), name, k)
            for i, q in enumerate(moved):
                blocks[q] = come[i]
        return blocks[1:]

    far = [jnp.concatenate([line[q:q + 1], cross[:, q - 1]]) for q in range(1, lines)]
    near = [jnp.concatenate([plane[q - 1:q], cross[q - 1]]) for q in range(1, PLANE)]
    far, near = across([None] + far, "line"), across([None] + near, "plane")
    far = jnp.concatenate(near + far)
    every = [own, far]
    for e in range(1, cores):
        every += [go(own, core=e), go(far, core=e)]

    result = pl.pallas_call(
        functools.partial(place_kernel, sz),
        out_shape=jax.ShapeDtypeStruct((tile, chips // cores * tile), f32),
        in_specs=[smem] + [vmem] * len(every),
        out_specs=vmem,
        scratch_shapes=[pltpu.VMEM((chips, tile, tile), f32)],
        compiler_params=pltpu.CompilerParams(vmem_limit_bytes=24 * 2**20),
        name="place",
    )(owner, *every)
    return result[None]


def solution(mesh):
    placed = (P("occ", "aux", None, None, None), P("aux", None, None), P("occ", "aux", None), P())
    return jax.shard_map(
        local, mesh=mesh, in_specs=placed, out_specs=P("aux", None, "occ"), check_vma=False
    )
```
